128 devices in a mesh: dp: 4 (over y), expert: 16 (over z, x), tensor: 2 (over core).
Axes of the slice: x: 4, y: 4, z: 4, core: 2. Of those that a mesh axis runs over, the one named last changes fastest.
Arguments:
- tokens: bfloat16 [8192, 7168], P(('dp', 'expert')), parts along dimension 0, may hold values from -6 to 6
- route_expert: int32 [8192, 8], P(('dp', 'expert')), parts along dimension 0, may hold values from 0 to 15, all different within a row; in each aligned block of 128 rows (0 to 127, 128 to 255, ...) at most 72 rows name the same one
- route_weight: int32 [8192, 8], P(('dp', 'expert')), parts along dimension 0, may hold values from 1 to 4095
- gate_weight: bfloat16 [16, 7168, 1024], P('expert', None, 'tensor'), may hold values from -0.0625 to 0.0625
- up_weight: bfloat16 [16, 7168, 1024], P('expert', None, 'tensor'), may hold values from -0.0625 to 0.0625
- down_weight: bfloat16 [16, 1024, 7168], P('expert', 'tensor'), may hold values from -0.1875 to 0.1875
- gate_scale: float32 [16, 1024], P('expert', 'tensor'), may hold values from 0.5 to 2
- up_scale: float32 [16, 1024], P('expert', 'tensor'), may hold values from 0.5 to 2
- down_scale: float32 [16, 7168], P('expert'), may hold values from 0.5 to 2
Outputs:
- combined: bfloat16 [8192, 7168], P(('dp', 'expert'), 'tensor'), parts along dimension 0
The draws below stay inside these ranges and needn't reach their ends.
There are 4 independent parts, one for each index of `dp`. The reference program is written for one: setup_inputs(seed, part) draws one part's arguments, and reference() takes and returns one part's arrays. A program takes and returns all parts, laid end to end along the dimension named above; an argument that names none is the same for every part. Nothing has to cross between parts.
Inputs may be any that keep to these rules, and one draw needn't show every extreme that they name: `route_expert`: within the 128 rows of one index of expert each expert is named at most 72 times, a bound that some block reaches; a token names 8 different experts.
All inputs are finite; a program needn't handle non-finite values.
Results may differ from the reference program's by a relative error of at most 0.0057.
Values may be sent and summed in bfloat16 or wider, within the bound.
A program may use at most 192 MiB of HBM per device.

```python
import math
import jax
import jax.numpy as jnp
import numpy as np
from jax import lax

D = 7168
FF = 1024
TOP = 8
EXPERTS = 16
TOK_DEV = 128
CAP = 72
TOKENS = 2048
N_EXPERT = 16


def set_ends(result, key, low, largest):
    extent = result.shape
    place = [jax.random.randint(jax.random.fold_in(key, axis), (), 0, extent[axis]) for axis in range(len(extent))]
    result = result.at[tuple(place)].set(low)
    longest = extent.index(max(extent))
    place[longest] = (place[longest] + 1) % extent[longest]
    return result.at[tuple(place)].set(largest)


def shard_levels(own_key, shape, split, least, top_value):
    level = 1.0
    for dim, blocks in split:
        steps = jax.random.uniform(jax.random.fold_in(jax.random.fold_in(own_key, 6), dim), (blocks,), jnp.float32, least / len(split), top_value / len(split))
        level = level * jnp.repeat(jnp.exp(steps), shape[dim] // blocks).reshape((-1,) + (1,) * (len(shape) - 1 - dim))
    return level


def shared_out(stream_key, own, number, rows, number_of, top, most, skew):
    order = jax.random.permutation(stream_key, number_of)
    heavy_load, usual = portions_of(number_of, rows * top, most, skew, True), portions_of(number_of, rows * top, most, skew, False)
    places = jnp.arange(number_of)

    def named(sizes, offset_by):
        used = int((sizes > 0).sum())
        fixed = max(1, used // 4)
        passed = fixed + (places - fixed + offset_by * (used - fixed)) % max(1, number_of - fixed)
        return jnp.zeros((number_of,), jnp.int32).at[order[jnp.where(places < fixed, places, passed)]].set(jnp.asarray(sizes, jnp.int32))

    sizes = jnp.where(number % 4 == 0, named(heavy_load, number // 4), named(usual, number - number // 4 - 1))
    mixed = jax.random.permutation(jax.random.fold_in(own, 3), number_of)
    donor, taker = mixed[0:number_of // 2 * 2:2], mixed[1:number_of // 2 * 2:2]
    room = jnp.minimum(sizes[donor] - 1, most - sizes[taker]) // 2
    room = jnp.where((donor == order[0]) | (taker == order[0]) | (sizes[taker] == 0), 0, jnp.maximum(room, 0))
    passed = jax.random.randint(jax.random.fold_in(own, 4), (number_of // 2,), 0, 1 << 20) % (room + 1)
    sizes = sizes.at[donor].add(-passed).at[taker].add(passed)
    labels = jnp.searchsorted(jnp.cumsum(sizes), jnp.arange(rows * top), side="right").astype(jnp.int32)
    table = labels.reshape(top, rows).T
    table = table[jax.random.permutation(jax.random.fold_in(own, 1), rows)]
    offset_by = jax.random.randint(jax.random.fold_in(own, 2), (rows, 1), 0, top)
    return jnp.take_along_axis(table, (jnp.arange(top)[None, :] + offset_by) % top, axis=1)


def portions_of(count, total, reach, skew, full):
    weights = [(1 << 20) // math.isqrt(grade ** skew) + 1 for grade in range(1, count + 1)]
    largest = reach if full else min(reach, max(-(-total // count), total * weights[0] // sum(weights)))
    least = 1 if total - largest >= count - 1 else 0
    counts, spare = [largest] + [least] * (count - 1), total - largest - least * (count - 1)
    while spare > 0:
        candidates = [i for i in range(1, count) if counts[i] < largest] or [i for i in range(1, count) if counts[i] < reach]
        pool, remaining = sum([weights[i] for i in candidates]), spare
        for i in candidates:
            more = min(reach - counts[i], max(1, remaining * weights[i] // pool), spare)
            counts[i] = counts[i] + more
            spare = spare - more
    return np.array(counts)


def bell_draw(rng, dims, spread, reach, shards=(), kind=jnp.bfloat16):
    array = spread * jax.random.normal(rng, dims, jnp.float32)
    if shards:
        array = array * shard_levels(rng, dims, shards, -0.22, 0.18)
    return jnp.clip(array, -reach, reach).astype(kind)


def setup_inputs(seed: int = 0, part: int = 0) -> dict:
    key_of = jax.random.split(jax.random.key(seed), 10)
    part_keys = jax.random.split(jax.random.fold_in(key_of[9], part), 10)
    tokens = bell_draw(part_keys[0], (TOKENS, D), 1.0, 6.0, ((0, 16),))
    route_expert_keys = jax.random.split(jax.random.fold_in(part_keys[1], 1), TOKENS // TOK_DEV)
    route_expert_turns = jax.random.permutation(jax.random.fold_in(part_keys[1], 3), TOKENS // TOK_DEV)
    route_expert = jax.vmap(lambda own, number: shared_out(jax.random.fold_in(part_keys[1], 2), own, number, TOK_DEV, EXPERTS, TOP, CAP, 2))(route_expert_keys, route_expert_turns).reshape((TOKENS, TOP))
    route_weight = set_ends(jax.random.randint(part_keys[2], (TOKENS, TOP), 1, 4096), jax.random.fold_in(part_keys[2], 1), 1, 4095).astype(jnp.int32)
    gate_weight = bell_draw(key_of[3], (EXPERTS, D, FF), D ** -0.5, 0.0625, ((0, 16), (2, 2)))
    up_weight = bell_draw(key_of[4], (EXPERTS, D, FF), D ** -0.5, 0.0625, ((0, 16), (2, 2)))
    down_weight = bell_draw(key_of[5], (EXPERTS, FF, D), FF ** -0.5, 0.1875, ((0, 16), (1, 2)))
    gate_scale = jnp.clip(jnp.exp(math.log(2.0) - 1.3862944 * jax.random.uniform(key_of[6], (EXPERTS, FF), jnp.float32) ** shard_levels(key_of[6], (EXPERTS, FF), ((0, 16), (1, 2)), -0.2, 0.2)), 0.5, 2.0)
    up_scale = jnp.clip(jnp.exp(math.log(2.0) - 1.3862944 * jax.random.uniform(key_of[7], (EXPERTS, FF), jnp.float32) ** shard_levels(key_of[7], (EXPERTS, FF), ((0, 16), (1, 2)), -0.2, 0.2)), 0.5, 2.0)
    down_scale = jnp.clip(jnp.exp(math.log(2.0) - 1.3862944 * jax.random.uniform(key_of[8], (EXPERTS, D), jnp.float32) ** shard_levels(key_of[8], (EXPERTS, D), ((0, 16),), -0.2, 0.2)), 0.5, 2.0)
    return {"tokens": tokens, "route_expert": route_expert, "route_weight": route_weight, "gate_weight": gate_weight, "up_weight": up_weight, "down_weight": down_weight, "gate_scale": gate_scale, "up_scale": up_scale, "down_scale": down_scale}


ROUTE_SCALE = 2.5


def slot_numbers(route_block, experts):
    flat_ids = route_block.reshape(-1).astype(jnp.int32)
    one_hot = (flat_ids[:, None] == jnp.arange(experts, dtype=jnp.int32)[None, :]).astype(jnp.int32)
    earlier = (jnp.cumsum(one_hot, axis=0) - one_hot).astype(jnp.int32)
    return jnp.sum(earlier * one_hot, axis=1).astype(jnp.int32).reshape(route_block.shape)


def reference(tokens, route_expert, route_weight, gate_weight, up_weight, down_weight, gate_scale, up_scale, down_scale):
    blocks = N_EXPERT
    total_rows = TOK_DEV * blocks
    route_blocks = route_expert.reshape(blocks, TOK_DEV, TOP)

    def block_slots(block_ids):
        return slot_numbers(block_ids, EXPERTS)

    slots = jax.vmap(block_slots)(route_blocks).reshape(total_rows, TOP).astype(jnp.int32)
    block_of = (jnp.arange(total_rows, dtype=jnp.int32) // TOK_DEV)[:, None]
    target = (route_expert.astype(jnp.int32) * (blocks * CAP) + block_of * CAP + slots).astype(jnp.int32)
    token_ids = jnp.repeat(jnp.arange(total_rows, dtype=jnp.int32), TOP)
    table = jnp.full((EXPERTS * blocks * CAP,), total_rows, jnp.int32).at[target.reshape(-1)].set(token_ids)
    padded = jnp.concatenate([tokens, jnp.zeros((1, D), jnp.bfloat16)], axis=0)

    def one_expert(operands):
        index_row, w_gate, w_up, w_down, s_gate, s_up, s_down = operands
        rows_in = padded[index_row]
        gate_act = jnp.dot(rows_in, w_gate, preferred_element_type=jnp.float32) * s_gate[None, :]
        up_act = jnp.dot(rows_in, w_up, preferred_element_type=jnp.float32) * s_up[None, :]
        hidden = (jax.nn.silu(gate_act) * up_act).astype(jnp.bfloat16)
        return (jnp.dot(hidden, w_down, preferred_element_type=jnp.float32) * s_down[None, :]).astype(jnp.bfloat16)

    outputs = lax.map(one_expert, (table.reshape(EXPERTS, blocks * CAP), gate_weight, up_weight, down_weight, gate_scale, up_scale, down_scale))
    flat_out = outputs.reshape(EXPERTS * blocks * CAP, D)
    weights_f = route_weight.astype(jnp.float32)
    mix = ROUTE_SCALE * weights_f / jnp.sum(weights_f, axis=1, keepdims=True)
    combined = jnp.zeros((total_rows, D), jnp.float32)
    for route_slot in range(TOP):
        combined = combined + mix[:, route_slot:route_slot + 1] * flat_out[target[:, route_slot]].astype(jnp.float32)
    return combined.astype(jnp.bfloat16)
```

```python
import jax
import jax.numpy as jnp
from jax import lax
from jax.experimental import pallas as pl
from jax.experimental.pallas import tpu as pltpu
from jax.sharding import PartitionSpec as P

ROUTE_SCALE = 2.5
MESH = pl.DeviceIdType.MESH
SIDE = 4
TOK = 128
CAP = 72
PAIR = 2 * CAP
OFFSETS = (0, 1, 3, 2)
BF16 = jnp.bfloat16
F32 = jnp.float32


def kernel(
    tok_hbm,
    re_ref,
    rw_ref,
    wg_hbm,
    wu_hbm,
    wd_hbm,
    sg_ref,
    su_ref,
    sd_ref,
    out_hbm,
    x_buf,
    wg,
    wu,
    wd,
    tok,
    send,
    ret,
    hid,
    own,
    part_in,
    info,
    pick,
    mix_hi,
    mix_lo,
    loc_sem,
    tok_s,
    tok_r,
    info_s,
    info_r,
    x_s,
    x_r,
    sib_s,
    sib_r,
    hid_s,
    hid_r,
    y_s,
    y_r,
    part_s,
    part_r,
    wd_sem,
):
    half = tok.shape[2]
    ff = wg.shape[1]
    d = lax.axis_index("dp")
    e = lax.axis_index("expert")
    c = lax.axis_index("tensor")
    z, x = e // SIDE, e % SIDE
    odd = (z + x) % 2

    def spot(axis, off):
        along_x = odd if axis == 0 else 1 - odd
        nz = (z + (1 - along_x) * off) % SIDE
        nx = (x + along_x * off) % SIDE
        return nz * SIDE + nx

    def dev(axis, off):
        return (d, spot(axis, off), c)

    sibling = (d, e, 1 - c)
    mine = pl.ds(pl.multiple_of(c * half, 128), half)
    other = pl.ds(pl.multiple_of((1 - c) * half, 128), half)
    hid_mine = pl.ds(pl.multiple_of(c * ff, 128), ff)

    def remote(src, dst, ss, rs, to):
        return pltpu.make_async_remote_copy(
            src_ref=src, dst_ref=dst, send_sem=ss, recv_sem=rs, device_id=to, device_id_type=MESH
        )

    tok_load = pltpu.make_async_copy(tok_hbm.at[:, mine], tok.at[0, 0:TOK], loc_sem.at[0])
    wg_load = pltpu.make_async_copy(wg_hbm.at[0], wg, loc_sem.at[1])
    wu_load = pltpu.make_async_copy(wu_hbm.at[0], wu, loc_sem.at[2])
    wd_load = pltpu.make_async_copy(
        wd_hbm.at[0, :, mine], wd.at[hid_mine], loc_sem.at[3]
    )
    tok_load.start()

    peers = [dev(a, o) for a in (0, 1) for o in (1, 3, 2)] + [sibling]
    barrier = pltpu.get_barrier_semaphore()
    for to in peers:
        pl.semaphore_signal(barrier, inc=1, device_id=to, device_id_type=MESH)
    pl.semaphore_wait(barrier, len(peers))

    tok_dst = (tok.at[1, 0:TOK], tok.at[1, TOK : 2 * TOK], tok.at[0, TOK : 2 * TOK])
    tok_cp = [
        remote(tok_hbm.at[:, mine], tok_dst[i], tok_s.at[i], tok_r.at[i], dev(0, (1, 3, 2)[i]))
        for i in range(3)
    ]
    for cp in tok_cp:
        cp.start()
    wg_load.start()
    wu_load.start()
    wd_load.start()
    wd_cp = remote(
        wd_hbm.at[0, :, other], wd.at[hid_mine], wd_sem.at[0], wd_sem.at[1], sibling
    )
    wd_cp.start()

    lane = lax.broadcasted_iota(jnp.int32, (TOK, TOK), 1)
    row = lax.broadcasted_iota(jnp.int32, (TOK, TOK), 0)
    wf = rw_ref[...].astype(F32)
    mix = ROUTE_SCALE * wf / jnp.sum(wf, axis=1, keepdims=True)
    chosen = jnp.zeros((TOK, TOK), F32)
    weight = jnp.zeros((TOK, TOK), F32)
    for k in range(re_ref.shape[1]):
        hit = re_ref[:, k : k + 1] == lane
        chosen = chosen + jnp.where(hit, 1.0, 0.0)
        weight = weight + jnp.where(hit, mix[:, k : k + 1], 0.0)
    chosen_t = chosen.T
    weight_t = weight.T
    before = jnp.where(row < lane, 1.0, 0.0).astype(BF16)
    place_t = jnp.dot(chosen_t.astype(BF16), before, preferred_element_type=F32)
    place_t = jnp.where(chosen_t > 0.5, place_t, -1.0)
    info[0, 0:16] = place_t[0:16]
    info[0, 16:32] = weight_t[0:16]
    info_cp = [
        remote(
            info.at[0],
            info.at[(2, 3, 1)[i]],
            info_s.at[i],
            info_r.at[i],
            dev(0, (1, 3, 2)[i]),
        )
        for i in range(3)
    ]
    for cp in info_cp:
        cp.start()
    for cp in info_cp:
        cp.wait_recv()

    slot_iota = lax.broadcasted_iota(jnp.int32, (PAIR, 2 * TOK), 0).astype(F32)

    def rows_of(pair, q):
        ex = spot(1 - pair, OFFSETS[q])
        first = info[2 * pair, pl.ds(ex, 1), :]
        second = info[2 * pair + 1, pl.ds(ex, 1), :]
        second = jnp.where(second >= 0.0, second + float(CAP), -1.0)
        return jnp.concatenate([first, second], axis=1)

    for pair in range(2):
        for q in range(4):
            rows = rows_of(pair, q)
            sel = jnp.where(slot_iota == rows, 1.0, 0.0)
            pick[pair, q * PAIR : (q + 1) * PAIR] = sel.astype(BF16)

    tile = 256

    def gather(pair):
        self_rows = pl.ds((1 - pair) * PAIR, PAIR)

        def step(n, carry):
            cols = pl.ds(pl.multiple_of(n * tile, tile), tile)
            got = jnp.dot(pick[pair], tok[pair, :, cols], preferred_element_type=F32).astype(BF16)
            home = pl.ds(pl.multiple_of(c * half + n * tile, 128), tile)
            x_buf[0, self_rows, home] = got[0:PAIR]
            send[pair, :, cols] = got[PAIR:]
            return carry

        lax.fori_loop(0, half // tile, step, 0)

    def part_at(pair, q):
        return pair if q < 3 else 1 - pair

    x_cp = {}
    for pair in range(2):
        for q in range(1, 4):
            part = part_at(pair, q)
            x_cp[pair, q] = remote(
                send.at[pair, (q - 1) * PAIR : q * PAIR],
                x_buf.at[q, part * PAIR : (part + 1) * PAIR, mine],
                x_s.at[pair * 3 + q - 1],
                x_r.at[2 * (q - 1) + part],
                dev(1 - pair, OFFSETS[q]),
            )
    sib_cp = {}
    for s in range(4):
        for part in range(2):
            at = x_buf.at[s, part * PAIR : (part + 1) * PAIR, mine]
            sib_cp[s, part] = remote(
                at, at, sib_s.at[2 * s + part], sib_r.at[2 * s + part], sibling
            )

    tok_cp[0].wait_recv()
    tok_cp[1].wait_recv()
    gather(1)
    for q in (1, 2, 3):
        x_cp[1, q].start()
    sib_cp[0, 0].start()
    tok_load.wait()
    tok_cp[2].wait_recv()
    gather(0)
    for q in (1, 2, 3):
        x_cp[0, q].start()
    sib_cp[0, 1].start()

    for pair in range(2):
        blocks = []
        for q in range(4):
            rows = rows_of(pair, q)
            ex = spot(1 - pair, OFFSETS[q])
            w = jnp.concatenate(
                [
                    info[2 * pair, pl.ds(16 + ex, 1), :],
                    info[2 * pair + 1, pl.ds(16 + ex, 1), :],
                ],
                axis=1,
            )
            blocks.append(jnp.where(slot_iota == rows, w, 0.0))
        blocks.append(jnp.zeros((mix_hi.shape[2] - 4 * PAIR, 2 * TOK), F32))
        full = jnp.concatenate(blocks, axis=0).T
        hi = full.astype(BF16)
        mix_hi[pair] = hi
        mix_lo[pair] = (full - hi.astype(F32)).astype(BF16)

    wg_load.wait()
    wu_load.wait()

    y_cp = {}
    back = (0, 3, 1, 2)
    for s in range(1, 4):
        for part in range(2):
            to = dev(part, back[s])
            pair = part_at(part, s)
            y_cp[s, part] = remote(
                x_buf.at[s, part * PAIR : (part + 1) * PAIR, other],
                ret.at[pair, s * PAIR : (s + 1) * PAIR],
                y_s.at[2 * (s - 1) + part],
                y_r.at[pair * 3 + s - 1],
                to,
            )
    hid_tile = 256
    for s in range(4):
        if s > 0:
            for part in range(2):
                x_cp[part_at(part, s), s].wait_recv()
                sib_cp[s, part].start()
        for part in range(2):
            sib_cp[s, part].wait()
        slot = s % 2

        def gate_up(n, carry):
            cols = pl.ds(pl.multiple_of(n * hid_tile, hid_tile), hid_tile)
            rows = x_buf[s]
            g = jnp.dot(rows, wg[:, cols], preferred_element_type=F32) * sg_ref[0:1, cols]
            u = jnp.dot(rows, wu[:, cols], preferred_element_type=F32) * su_ref[0:1, cols]
            h = (g / (1.0 + jnp.exp(-g))) * u
            at = pl.ds(pl.multiple_of(c * ff + n * hid_tile, 128), hid_tile)
            hid[slot, :, at] = h.astype(BF16)
            return carry

        lax.fori_loop(0, ff // hid_tile, gate_up, 0)
        hid_cp = remote(
            hid.at[slot, :, hid_mine],
            hid.at[slot, :, hid_mine],
            hid_s.at[s],
            hid_r.at[s],
            sibling,
        )
        hid_cp.start()
        if s == 0:
            wd_load.wait()
            wd_cp.wait()
        hid_cp.wait()

        def down(n, carry):
            cols = pl.ds(pl.multiple_of(n * tile, tile), tile)
            scale_at = pl.ds(pl.multiple_of(c * half + n * tile, 128), tile)
            y = jnp.dot(hid[slot], wd[:, cols], preferred_element_type=F32)
            y = (y * sd_ref[0:1, scale_at]).astype(BF16)
            if s == 0:
                ret[1, 0:PAIR, cols] = y[0:PAIR]
                ret[0, 0:PAIR, cols] = y[PAIR:]
            else:
                at = pl.ds(pl.multiple_of((1 - c) * half + n * tile, 128), tile)
                x_buf[s, :, at] = y
            return carry

        lax.fori_loop(0, half // tile, down, 0)
        if s > 0:
            for part in range(2):
                y_cp[s, part].start()

    for cp in tok_cp + info_cp:
        cp.wait_send()

    def combine(pair):
        def step(n, carry):
            cols = pl.ds(pl.multiple_of(n * tile, tile), tile)
            rows = ret[pair, :, cols]
            k = rows.shape[0]
            total = jnp.dot(mix_hi[pair, :, 0:k], rows, preferred_element_type=F32)
            total = total + jnp.dot(mix_lo[pair, :, 0:k], rows, preferred_element_type=F32)
            if pair == 0:
                own[:, cols] = total[0:TOK]
                tok[0, TOK:, cols] = total[TOK:].astype(BF16)
            else:
                tok[1, :, cols] = total.astype(BF16)
            return carry

        lax.fori_loop(0, half // tile, step, 0)

    part_cp = [
        remote(tok.at[1, 0:TOK], part_in.at[0], part_s.at[0], part_r.at[0], dev(1, 3)),
        remote(tok.at[1, TOK : 2 * TOK], part_in.at[1], part_s.at[1], part_r.at[1], dev(1, 1)),
        remote(tok.at[0, TOK : 2 * TOK], part_in.at[2], part_s.at[2], part_r.at[2], dev(0, 2)),
    ]

    def wait_rows(pair):
        for q in range(1, 4):
            y_cp[q, part_at(pair, q)].wait_recv()

    wait_rows(1)
    combine(1)
    part_cp[0].start()
    part_cp[1].start()
    wait_rows(0)
    combine(0)
    part_cp[2].start()
    for cp in part_cp:
        cp.wait_recv()

    def finish(n, carry):
        cols = pl.ds(pl.multiple_of(n * tile, tile), tile)
        total = own[:, cols]
        for i in range(3):
            total = total + part_in[i, :, cols].astype(F32)
        tok[0, 0:TOK, cols] = total.astype(BF16)
        return carry

    lax.fori_loop(0, half // tile, finish, 0)
    store = pltpu.make_async_copy(tok.at[0, 0:TOK], out_hbm, loc_sem.at[4])
    store.start()
    for cp in list(x_cp.values()) + list(y_cp.values()) + part_cp:
        cp.wait_send()
    store.wait()


def body(
    tokens,
    route_expert,
    route_weight,
    gate_weight,
    up_weight,
    down_weight,
    gate_scale,
    up_scale,
    down_scale,
):
    rows, width = tokens.shape
    half = width // 2
    ff = gate_weight.shape[2]
    hbm = pl.BlockSpec(memory_space=pl.ANY)
    vmem = pl.BlockSpec(memory_space=pltpu.VMEM)
    dma = pltpu.SemaphoreType.DMA
    return pl.pallas_call(
        kernel,
        out_shape=jax.ShapeDtypeStruct((rows, half), BF16),
        in_specs=[hbm, vmem, vmem, hbm, hbm, hbm, vmem, vmem, vmem],
        out_specs=hbm,
        scratch_shapes=[
            pltpu.VMEM((4, 2 * PAIR, width), BF16),
            pltpu.VMEM((width, ff), BF16),
            pltpu.VMEM((width, ff), BF16),
            pltpu.VMEM((2 * ff, half), BF16),
            pltpu.VMEM((2, 2 * TOK, half), BF16),
            pltpu.VMEM((2, 3 * PAIR, half), BF16),
            pltpu.VMEM((2, 4 * PAIR, half), BF16),
            pltpu.VMEM((2, 2 * PAIR, 2 * ff), BF16),
            pltpu.VMEM((TOK, half), F32),
            pltpu.VMEM((3, TOK, half), BF16),
            pltpu.VMEM((4, 32, TOK), F32),
            pltpu.VMEM((2, 4 * PAIR, 2 * TOK), BF16),
            pltpu.VMEM((2, 2 * TOK, 640), BF16),
            pltpu.VMEM((2, 2 * TOK, 640), BF16),
            dma((5,)),
            dma((3,)),
            dma((3,)),
            dma((3,)),
            dma((3,)),
            dma((6,)),
            dma((6,)),
            dma((8,)),
            dma((8,)),
            dma((4,)),
            dma((4,)),
            dma((6,)),
            dma((6,)),
            dma((3,)),
            dma((3,)),
            dma((2,)),
        ],
        compiler_params=pltpu.CompilerParams(
            collective_id=0, has_side_effects=True, vmem_limit_bytes=63 * 2**20
        ),
        name="routed_ffn",
    )(
        tokens,
        route_expert,
        route_weight,
        gate_weight,
        up_weight,
        down_weight,
        gate_scale,
        up_scale,
        down_scale,
    )


def solution(mesh):
    in_specs = (
        P(("dp", "expert"), None),
        P(("dp", "expert"), None),
        P(("dp", "expert"), None),
        P("expert", None, "tensor"),
        P("expert", None, "tensor"),
        P("expert", "tensor", None),
        P("expert", "tensor"),
        P("expert", "tensor"),
        P("expert", None),
    )
    out_specs = P(("dp", "expert"), "tensor")
    return jax.shard_map(body, mesh=mesh, in_specs=in_specs, out_specs=out_specs, check_vma=False)
```

```python
import jax
import jax.numpy as jnp
from jax import lax
from jax.experimental import pallas as pl
from jax.experimental.pallas import tpu as pltpu
from jax.sharding import PartitionSpec as P

ROUTE_SCALE = 2.5
MESH = pl.DeviceIdType.MESH
SIDE = 4
TOK = 128
CAP = 72
PAIR = 2 * CAP
OFFSETS = (0, 1, 3, 2)
BF16 = jnp.bfloat16
F32 = jnp.float32


def kernel(
    tok_hbm,
    re_ref,
    rw_ref,
    wg_hbm,
    wu_hbm,
    wd_hbm,
    sg_ref,
    su_ref,
    sd_ref,
    out_hbm,
    x_buf,
    wg,
    wu,
    wd,
    tok,
    send,
    ret,
    hid,
    own,
    part_in,
    relay,
    info,
    pick,
    mix_hi,
    mix_lo,
    loc_sem,
    tok_s,
    tok_r,
    info_s,
    info_r,
    x_s,
    x_r,
    sib_s,
    sib_r,
    hid_s,
    hid_r,
    y_s,
    y_r,
    part_s,
    part_r,
    relay_s,
    relay_r,
    wd_sem,
):
    half = tok.shape[2]
    ff = wg.shape[1]
    d = lax.axis_index("dp")
    e = lax.axis_index("expert")
    c = lax.axis_index("tensor")
    z, x = e // SIDE, e % SIDE
    odd = (z + x) % 2

    def spot(axis, off):
        along_x = odd if axis == 0 else 1 - odd
        nz = (z + (1 - along_x) * off) % SIDE
        nx = (x + along_x * off) % SIDE
        return nz * SIDE + nx

    def dev(axis, off):
        return (d, spot(axis, off), c)

    sibling = (d, e, 1 - c)
    mine = pl.ds(pl.multiple_of(c * half, 128), half)
    other = pl.ds(pl.multiple_of((1 - c) * half, 128), half)
    hid_mine = pl.ds(pl.multiple_of(c * ff, 128), ff)

    def remote(src, dst, ss, rs, to):
        return pltpu.make_async_remote_copy(
            src_ref=src, dst_ref=dst, send_sem=ss, recv_sem=rs, device_id=to, device_id_type=MESH
        )

    tok_load = pltpu.make_async_copy(tok_hbm.at[:, mine], tok.at[0, 0:TOK], loc_sem.at[0])
    wg_load = pltpu.make_async_copy(wg_hbm.at[0], wg, loc_sem.at[1])
    wu_load = pltpu.make_async_copy(wu_hbm.at[0], wu, loc_sem.at[2])
    wd_load = pltpu.make_async_copy(
        wd_hbm.at[0, :, mine], wd.at[hid_mine], loc_sem.at[3]
    )
    tok_load.start()

    peers = [dev(a, o) for a in (0, 1) for o in (1, 3, 2)] + [sibling]
    barrier = pltpu.get_barrier_semaphore()
    for to in peers:
        pl.semaphore_signal(barrier, inc=1, device_id=to, device_id_type=MESH)
    pl.semaphore_wait(barrier, len(peers))

    chunk = half // 2
    tile = 256
    big = -(-chunk // (2 * tile)) * tile
    ends = (0, big, chunk, 2 * chunk - big, half)
    quarter = [pl.ds(ends[q], ends[q + 1] - ends[q]) for q in range(4)]
    chunks = [pl.ds(k * chunk, chunk) for k in range(2)]

    tok_cp = {}
    for i, off in enumerate((1, 3)):
        for q in range(4):
            tok_cp[i, q] = remote(
                tok_hbm.at[:, pl.ds(pl.multiple_of(c * half + ends[q], 128), ends[q + 1] - ends[q])],
                tok.at[1, i * TOK : (i + 1) * TOK, quarter[q]],
                tok_s.at[4 * i + q],
                tok_r.at[4 * i + q],
                dev(0, off),
            )
    for q in range(4):
        tok_cp[0, q].start()
        tok_cp[1, q ^ 1].start()
    for q in range(4):
        side = q % 2
        tok_cp[2, q] = remote(
            tok.at[1, side * TOK : (side + 1) * TOK, quarter[q]],
            tok.at[0, TOK : 2 * TOK, quarter[q]],
            tok_s.at[8 + q],
            tok_r.at[8 + q],
            dev(1, (1, 3)[side]),
        )
    wg_load.start()
    wu_load.start()
    wd_load.start()
    wd_cp = remote(
        wd_hbm.at[0, :, other], wd.at[hid_mine], wd_sem.at[0], wd_sem.at[1], sibling
    )
    wd_cp.start()

    lane = lax.broadcasted_iota(jnp.int32, (TOK, TOK), 1)
    row = lax.broadcasted_iota(jnp.int32, (TOK, TOK), 0)
    wf = rw_ref[...].astype(F32)
    mix = ROUTE_SCALE * wf / jnp.sum(wf, axis=1, keepdims=True)
    chosen = jnp.zeros((TOK, TOK), F32)
    weight = jnp.zeros((TOK, TOK), F32)
    for k in range(re_ref.shape[1]):
        hit = re_ref[:, k : k + 1] == lane
        chosen = chosen + jnp.where(hit, 1.0, 0.0)
        weight = weight + jnp.where(hit, mix[:, k : k + 1], 0.0)
    chosen_t = chosen.T
    weight_t = weight.T
    before = jnp.where(row < lane, 1.0, 0.0).astype(BF16)
    place_t = jnp.dot(chosen_t.astype(BF16), before, preferred_element_type=F32)
    place_t = jnp.where(chosen_t > 0.5, place_t, -1.0)
    info[0, 0:16] = place_t[0:16]
    info[0, 16:32] = weight_t[0:16]
    info_cp = [
        remote(
            info.at[0],
            info.at[(2, 3, 1)[i]],
            info_s.at[i],
            info_r.at[i],
            dev(0, (1, 3, 2)[i]),
        )
        for i in range(3)
    ]
    for cp in info_cp:
        cp.start()
    for cp in info_cp:
        cp.wait_recv()

    slot_iota = lax.broadcasted_iota(jnp.int32, (PAIR, 2 * TOK), 0).astype(F32)

    def rows_of(pair, q):
        ex = spot(1 - pair, OFFSETS[q])
        first = info[2 * pair, pl.ds(ex, 1), :]
        second = info[2 * pair + 1, pl.ds(ex, 1), :]
        second = jnp.where(second >= 0.0, second + float(CAP), -1.0)
        return jnp.concatenate([first, second], axis=1)

    for pair in range(2):
        for q in range(4):
            rows = rows_of(pair, q)
            sel = jnp.where(slot_iota == rows, 1.0, 0.0)
            pick[pair, q * PAIR : (q + 1) * PAIR] = sel.astype(BF16)

    def gather(pair, k):
        self_rows = pl.ds((1 - pair) * PAIR, PAIR)

        def step(n, carry):
            cols = pl.ds(pl.multiple_of(n * tile, tile), tile)
            got = jnp.dot(pick[pair], tok[pair, :, cols], preferred_element_type=F32).astype(BF16)
            home = pl.ds(pl.multiple_of(c * half + n * tile, 128), tile)
            x_buf[0, self_rows, home] = got[0:PAIR]
            send[pair, :, cols] = got[PAIR:]
            return carry

        lax.fori_loop(k * chunk // tile, (k + 1) * chunk // tile, step, 0)

    def part_at(pair, q):
        return pair if q < 3 else 1 - pair

    x_cp = {}
    for pair in range(2):
        for q in range(1, 4):
            part = part_at(pair, q)
            for k in range(2):
                home = pl.ds(pl.multiple_of(c * half + k * chunk, 128), chunk)
                x_cp[pair, q, k] = remote(
                    send.at[pair, (q - 1) * PAIR : q * PAIR, chunks[k]],
                    x_buf.at[q, part * PAIR : (part + 1) * PAIR, home],
                    x_s.at[2 * (pair * 3 + q - 1) + k],
                    x_r.at[2 * (2 * (q - 1) + part) + k],
                    dev(1 - pair, OFFSETS[q]),
                )
    sib_cp = {}
    for s in range(4):
        for part in range(2):
            at = x_buf.at[s, part * PAIR : (part + 1) * PAIR, mine]
            sib_cp[s, part] = remote(
                at, at, sib_s.at[2 * s + part], sib_r.at[2 * s + part], sibling
            )

    for k in range(2):
        for side in range(2):
            tok_cp[side, 2 * k + side].wait_recv()
            tok_cp[2, 2 * k + side].start()
        for side in range(2):
            tok_cp[side, 2 * k + 1 - side].wait_recv()
        gather(1, k)
        for q in (1, 2):
            x_cp[1, q, k].start()
        if k == 0:
            tok_load.wait()
        else:
            sib_cp[0, 0].start()
        tok_cp[2, 2 * k].wait_recv()
        tok_cp[2, 2 * k + 1].wait_recv()
        gather(0, k)
        for q in (1, 2):
            x_cp[0, q, k].start()
    sib_cp[0, 1].start()
    for k in range(2):
        for pair in range(2):
            x_cp[pair, 3, k].start()

    for pair in range(2):
        blocks = []
        for q in range(4):
            rows = rows_of(pair, q)
            ex = spot(1 - pair, OFFSETS[q])
            w = jnp.concatenate(
                [
                    info[2 * pair, pl.ds(16 + ex, 1), :],
                    info[2 * pair + 1, pl.ds(16 + ex, 1), :],
                ],
                axis=1,
            )
            blocks.append(jnp.where(slot_iota == rows, w, 0.0))
        blocks.append(jnp.zeros((mix_hi.shape[2] - 4 * PAIR, 2 * TOK), F32))
        full = jnp.concatenate(blocks, axis=0).T
        hi = full.astype(BF16)
        mix_hi[pair] = hi
        mix_lo[pair] = (full - hi.astype(F32)).astype(BF16)

    wg_load.wait()
    wu_load.wait()

    y_cp = {}
    back = (0, 3, 1, 2)
    for s in range(1, 4):
        for part in range(2):
            pair = part_at(part, s)
            for k in range(2):
                away = pl.ds(pl.multiple_of((1 - c) * half + k * chunk, 128), chunk)
                y_cp[s, part, k] = remote(
                    x_buf.at[s, part * PAIR : (part + 1) * PAIR, away],
                    ret.at[pair, s * PAIR : (s + 1) * PAIR, chunks[k]],
                    y_s.at[2 * (2 * (s - 1) + part) + k],
                    y_r.at[2 * (pair * 3 + s - 1) + k],
                    dev(part, back[s]),
                )
    hid_tile = 256
    for s in range(4):
        if s > 0:
            for part in range(2):
                for k in range(2):
                    x_cp[part_at(part, s), s, k].wait_recv()
                sib_cp[s, part].start()
        for part in range(2):
            sib_cp[s, part].wait()
        slot = s % 2

        def gate_up(n, carry):
            cols = pl.ds(pl.multiple_of(n * hid_tile, hid_tile), hid_tile)
            rows = x_buf[s]
            g = jnp.dot(rows, wg[:, cols], preferred_element_type=F32) * sg_ref[0:1, cols]
            u = jnp.dot(rows, wu[:, cols], preferred_element_type=F32) * su_ref[0:1, cols]
            h = (g / (1.0 + jnp.exp(-g))) * u
            at = pl.ds(pl.multiple_of(c * ff + n * hid_tile, 128), hid_tile)
            hid[slot, :, at] = h.astype(BF16)
            return carry

        lax.fori_loop(0, ff // hid_tile, gate_up, 0)
        hid_cp = remote(
            hid.at[slot, :, hid_mine],
            hid.at[slot, :, hid_mine],
            hid_s.at[s],
            hid_r.at[s],
            sibling,
        )
        hid_cp.start()
        if s == 0:
            wd_load.wait()
            wd_cp.wait()
        hid_cp.wait()

        def down(n, carry):
            cols = pl.ds(pl.multiple_of(n * tile, tile), tile)
            scale_at = pl.ds(pl.multiple_of(c * half + n * tile, 128), tile)
            y = jnp.dot(hid[slot], wd[:, cols], preferred_element_type=F32)
            y = (y * sd_ref[0:1, scale_at]).astype(BF16)
            if s == 0:
                ret[1, 0:PAIR, cols] = y[0:PAIR]
                ret[0, 0:PAIR, cols] = y[PAIR:]
            else:
                at = pl.ds(pl.multiple_of((1 - c) * half + n * tile, 128), tile)
                x_buf[s, :, at] = y
            return carry

        for k in range(2):
            lax.fori_loop(k * chunk // tile, (k + 1) * chunk // tile, down, 0)
            if s > 0:
                for part in range(2):
                    y_cp[s, part, k].start()

    for cp in list(tok_cp.values()) + info_cp:
        cp.wait_send()

    def combine(pair, q):
        def step(n, carry):
            cols = pl.ds(pl.multiple_of(n * tile, tile), tile)
            rows = ret[pair, :, cols]
            depth = rows.shape[0]
            total = jnp.dot(mix_hi[pair, :, 0:depth], rows, preferred_element_type=F32)
            total = total + jnp.dot(mix_lo[pair, :, 0:depth], rows, preferred_element_type=F32)
            first, second = total[0:TOK], total[TOK:]
            if pair == 0:
                own[:, cols] = first
                tok[0, TOK:, cols] = second.astype(BF16)
            else:
                passed = relay[:, cols].astype(F32)
                if q % 2 == 0:
                    second = second + passed
                else:
                    first = first + passed
                tok[1, 0:TOK, cols] = first.astype(BF16)
                tok[1, TOK:, cols] = second.astype(BF16)
            return carry

        lax.fori_loop(ends[q] // tile, ends[q + 1] // tile, step, 0)

    relay_cp = [
        remote(
            tok.at[0, TOK : 2 * TOK, quarter[q]],
            relay.at[:, quarter[q]],
            relay_s.at[q],
            relay_r.at[q],
            dev(0, (1, 3)[q % 2]),
        )
        for q in range(4)
    ]
    part_cp = {}
    for i in range(2):
        for k in range(2):
            part_cp[i, k] = remote(
                tok.at[1, i * TOK : (i + 1) * TOK, chunks[k]],
                part_in.at[i, :, chunks[k]],
                part_s.at[2 * i + k],
                part_r.at[2 * i + k],
                dev(1, (3, 1)[i]),
            )

    def wait_rows(pair, k):
        for q in range(1, 4):
            y_cp[q, part_at(pair, q), k].wait_recv()

    for k in range(2):
        wait_rows(0, k)
        for q in (2 * k, 2 * k + 1):
            combine(0, q)
            relay_cp[q].start()
        wait_rows(1, k)
        for q in (2 * k, 2 * k + 1):
            relay_cp[q].wait_recv()
            combine(1, q)
        for i in range(2):
            part_cp[i, k].start()

    def finish(n, carry):
        cols = pl.ds(pl.multiple_of(n * tile, tile), tile)
        total = own[:, cols]
        for i in range(2):
            total = total + part_in[i, :, cols].astype(F32)
        tok[0, 0:TOK, cols] = total.astype(BF16)
        return carry

    stores = []
    for k in range(2):
        for i in range(2):
            part_cp[i, k].wait_recv()
        lax.fori_loop(k * chunk // tile, (k + 1) * chunk // tile, finish, 0)
        store = pltpu.make_async_copy(
            tok.at[0, 0:TOK, chunks[k]], out_hbm.at[:, chunks[k]], loc_sem.at[4 + k]
        )
        store.start()
        stores.append(store)
    for cp in [*x_cp.values(), *y_cp.values(), *part_cp.values(), *relay_cp]:
        cp.wait_send()
    for store in stores:
        store.wait()


def body(
    tokens,
    route_expert,
    route_weight,
    gate_weight,
    up_weight,
    down_weight,
    gate_scale,
    up_scale,
    down_scale,
):
    rows, width = tokens.shape
    half = width // 2
    ff = gate_weight.shape[2]
    hbm = pl.BlockSpec(memory_space=pl.ANY)
    vmem = pl.BlockSpec(memory_space=pltpu.VMEM)
    dma = pltpu.SemaphoreType.DMA
    return pl.pallas_call(
        kernel,
        out_shape=jax.ShapeDtypeStruct((rows, half), BF16),
        in_specs=[hbm, vmem, vmem, hbm, hbm, hbm, vmem, vmem, vmem],
        out_specs=hbm,
        scratch_shapes=[
            pltpu.VMEM((4, 2 * PAIR, width), BF16),
            pltpu.VMEM((width, ff), BF16),
            pltpu.VMEM((width, ff), BF16),
            pltpu.VMEM((2 * ff, half), BF16),
            pltpu.VMEM((2, 2 * TOK, half), BF16),
            pltpu.VMEM((2, 3 * PAIR, half), BF16),
            pltpu.VMEM((2, 4 * PAIR, half), BF16),
            pltpu.VMEM((2, 2 * PAIR, 2 * ff), BF16),
            pltpu.VMEM((TOK, half), F32),
            pltpu.VMEM((2, TOK, half), BF16),
            pltpu.VMEM((TOK, half), BF16),
            pltpu.VMEM((4, 32, TOK), F32),
            pltpu.VMEM((2, 4 * PAIR, 2 * TOK), BF16),
            pltpu.VMEM((2, 2 * TOK, 640), BF16),
            pltpu.VMEM((2, 2 * TOK, 640), BF16),
            dma((6,)),
            dma((12,)),
            dma((12,)),
            dma((3,)),
            dma((3,)),
            dma((12,)),
            dma((12,)),
            dma((8,)),
            dma((8,)),
            dma((4,)),
            dma((4,)),
            dma((12,)),
            dma((12,)),
            dma((4,)),
            dma((4,)),
            dma((4,)),
            dma((4,)),
            dma((2,)),
        ],
        compiler_params=pltpu.CompilerParams(
            collective_id=0, has_side_effects=True, vmem_limit_bytes=63 * 2**20
        ),
        name="routed_ffn",
    )(
        tokens,
        route_expert,
        route_weight,
        gate_weight,
        up_weight,
        down_weight,
        gate_scale,
        up_scale,
        down_scale,
    )


def solution(mesh):
    in_specs = (
        P(("dp", "expert"), None),
        P(("dp", "expert"), None),
        P(("dp", "expert"), None),
        P("expert", None, "tensor"),
        P("expert", None, "tensor"),
        P("expert", "tensor", None),
        P("expert", "tensor"),
        P("expert", "tensor"),
        P("expert", None),
    )
    out_specs = P(("dp", "expert"), "tensor")
    return jax.shard_map(body, mesh=mesh, in_specs=in_specs, out_specs=out_specs, check_vma=False)
```

```python
import jax
import jax.numpy as jnp
from jax import lax
from jax.experimental import pallas as pl
from jax.experimental.pallas import tpu as pltpu
from jax.sharding import PartitionSpec as P

ROUTE_SCALE = 2.5
MESH = pl.DeviceIdType.MESH
SIDE = 4
TOK = 128
CAP = 72
PAIR = 2 * CAP
OFFSETS = (0, 1, 3, 2)
BF16 = jnp.bfloat16
F32 = jnp.float32


def kernel(
    tok_hbm,
    re_ref,
    rw_ref,
    wg_hbm,
    wu_hbm,
    wd_hbm,
    sg_ref,
    su_ref,
    sd_ref,
    out_hbm,
    x_buf,
    wg,
    wu,
    wd,
    tok,
    send,
    ret,
    hid,
    own,
    part_in,
    relay,
    info,
    pick,
    mix_hi,
    mix_lo,
    loc_sem,
    tok_s,
    tok_r,
    info_s,
    info_r,
    x_s,
    x_r,
    sib_s,
    sib_r,
    hid_s,
    hid_r,
    y_s,
    y_r,
    part_s,
    part_r,
    relay_s,
    relay_r,
    wd_sem,
):
    half = tok.shape[2]
    ff = wg.shape[1]
    d = lax.axis_index("dp")
    e = lax.axis_index("expert")
    c = lax.axis_index("tensor")
    z, x = e // SIDE, e % SIDE
    odd = (z + x) % 2

    def spot(axis, off):
        along_x = odd if axis == 0 else 1 - odd
        nz = (z + (1 - along_x) * off) % SIDE
        nx = (x + along_x * off) % SIDE
        return nz * SIDE + nx

    def dev(axis, off):
        return (d, spot(axis, off), c)

    sibling = (d, e, 1 - c)
    mine = pl.ds(pl.multiple_of(c * half, 128), half)
    other = pl.ds(pl.multiple_of((1 - c) * half, 128), half)
    hid_mine = pl.ds(pl.multiple_of(c * ff, 128), ff)

    def remote(src, dst, ss, rs, to):
        return pltpu.make_async_remote_copy(
            src_ref=src, dst_ref=dst, send_sem=ss, recv_sem=rs, device_id=to, device_id_type=MESH
        )

    tok_load = pltpu.make_async_copy(tok_hbm.at[:, mine], tok.at[0, 0:TOK], loc_sem.at[0])
    wg_load = pltpu.make_async_copy(wg_hbm.at[0], wg, loc_sem.at[1])
    wu_load = pltpu.make_async_copy(wu_hbm.at[0], wu, loc_sem.at[2])
    wd_load = pltpu.make_async_copy(
        wd_hbm.at[0, :, mine], wd.at[hid_mine], loc_sem.at[3]
    )
    tok_load.start()

    peers = [dev(a, o) for a in (0, 1) for o in (1, 3, 2)] + [sibling]
    barrier = pltpu.get_barrier_semaphore()
    for to in peers:
        pl.semaphore_signal(barrier, inc=1, device_id=to, device_id_type=MESH)
    pl.semaphore_wait(barrier, len(peers))

    chunk = half // 2
    tile = 256
    big = -(-chunk // (2 * tile)) * tile
    ends = (0, big, chunk, 2 * chunk - big, half)
    quarter = [pl.ds(ends[q], ends[q + 1] - ends[q]) for q in range(4)]
    chunks = [pl.ds(k * chunk, chunk) for k in range(2)]

    tok_cp = {}
    for i, off in enumerate((1, 3)):
        for q in range(4):
            tok_cp[i, q] = remote(
                tok_hbm.at[:, pl.ds(pl.multiple_of(c * half + ends[q], 128), ends[q + 1] - ends[q])],
                tok.at[1, i * TOK : (i + 1) * TOK, quarter[q]],
                tok_s.at[4 * i + q],
                tok_r.at[4 * i + q],
                dev(0, off),
            )

    def next_quarter(q):
        if q > 0:
            tok_cp[0, q - 1].wait_send()
            tok_cp[1, (q - 1) ^ 1].wait_send()
        if q < 4:
            tok_cp[0, q].start()
            tok_cp[1, q ^ 1].start()

    next_quarter(0)
    for q in range(4):
        side = q % 2
        tok_cp[2, q] = remote(
            tok.at[1, side * TOK : (side + 1) * TOK, quarter[q]],
            tok.at[0, TOK : 2 * TOK, quarter[q]],
            tok_s.at[8 + q],
            tok_r.at[8 + q],
            dev(1, (1, 3)[side]),
        )
    wg_load.start()
    wu_load.start()
    wd_load.start()
    wd_cp = remote(
        wd_hbm.at[0, :, other], wd.at[hid_mine], wd_sem.at[0], wd_sem.at[1], sibling
    )
    wd_cp.start()

    lane = lax.broadcasted_iota(jnp.int32, (TOK, TOK), 1)
    row = lax.broadcasted_iota(jnp.int32, (TOK, TOK), 0)
    wf = rw_ref[...].astype(F32)
    mix = ROUTE_SCALE * wf / jnp.sum(wf, axis=1, keepdims=True)
    chosen = jnp.zeros((TOK, TOK), F32)
    weight = jnp.zeros((TOK, TOK), F32)
    for k in range(re_ref.shape[1]):
        hit = re_ref[:, k : k + 1] == lane
        chosen = chosen + jnp.where(hit, 1.0, 0.0)
        weight = weight + jnp.where(hit, mix[:, k : k + 1], 0.0)
    chosen_t = chosen.T
    weight_t = weight.T
    before = jnp.where(row < lane, 1.0, 0.0).astype(BF16)
    place_t = jnp.dot(chosen_t.astype(BF16), before, preferred_element_type=F32)
    place_t = jnp.where(chosen_t > 0.5, place_t, -1.0)
    info[0, 0:16] = place_t[0:16]
    info[0, 16:32] = weight_t[0:16]
    info_cp = [
        remote(
            info.at[0],
            info.at[(2, 3, 1)[i]],
            info_s.at[i],
            info_r.at[i],
            dev(0, (1, 3, 2)[i]),
        )
        for i in range(3)
    ]
    for cp in info_cp:
        cp.start()
    for cp in info_cp:
        cp.wait_recv()

    slot_iota = lax.broadcasted_iota(jnp.int32, (PAIR, 2 * TOK), 0).astype(F32)

    def rows_of(pair, q):
        ex = spot(1 - pair, OFFSETS[q])
        first = info[2 * pair, pl.ds(ex, 1), :]
        second = info[2 * pair + 1, pl.ds(ex, 1), :]
        second = jnp.where(second >= 0.0, second + float(CAP), -1.0)
        return jnp.concatenate([first, second], axis=1)

    for pair in range(2):
        for q in range(4):
            rows = rows_of(pair, q)
            sel = jnp.where(slot_iota == rows, 1.0, 0.0)
            pick[pair, q * PAIR : (q + 1) * PAIR] = sel.astype(BF16)

    def gather(pair, k):
        self_rows = pl.ds((1 - pair) * PAIR, PAIR)

        def step(n, carry):
            cols = pl.ds(pl.multiple_of(n * tile, tile), tile)
            got = jnp.dot(pick[pair], tok[pair, :, cols], preferred_element_type=F32).astype(BF16)
            home = pl.ds(pl.multiple_of(c * half + n * tile, 128), tile)
            x_buf[0, self_rows, home] = got[0:PAIR]
            send[pair, :, cols] = got[PAIR:]
            return carry

        lax.fori_loop(k * chunk // tile, (k + 1) * chunk // tile, step, 0)

    def part_at(pair, q):
        return pair if q < 3 else 1 - pair

    x_cp = {}
    for pair in range(2):
        for q in range(1, 4):
            part = part_at(pair, q)
            for k in range(2):
                home = pl.ds(pl.multiple_of(c * half + k * chunk, 128), chunk)
                x_cp[pair, q, k] = remote(
                    send.at[pair, (q - 1) * PAIR : q * PAIR, chunks[k]],
                    x_buf.at[q, part * PAIR : (part + 1) * PAIR, home],
                    x_s.at[2 * (pair * 3 + q - 1) + k],
                    x_r.at[2 * (2 * (q - 1) + part) + k],
                    dev(1 - pair, OFFSETS[q]),
                )
    sib_cp = {}
    for s in range(4):
        for part in range(2):
            at = x_buf.at[s, part * PAIR : (part + 1) * PAIR, mine]
            sib_cp[s, part] = remote(
                at, at, sib_s.at[2 * s + part], sib_r.at[2 * s + part], sibling
            )

    for k in range(2):
        next_quarter(2 * k + 1)
        for side in range(2):
            tok_cp[side, 2 * k + side].wait_recv()
            tok_cp[2, 2 * k + side].start()
        next_quarter(2 * k + 2)
        for side in range(2):
            tok_cp[side, 2 * k + 1 - side].wait_recv()
        if k == 1:
            for q in (1, 2):
                x_cp[1, q, 0].start()
        gather(1, k)
        if k == 1:
            sib_cp[0, 0].start()
            for q in (1, 2):
                x_cp[1, q, 1].start()
        else:
            tok_load.wait()
        tok_cp[2, 2 * k].wait_recv()
        tok_cp[2, 2 * k + 1].wait_recv()
        gather(0, k)
        for q in (1, 2):
            x_cp[0, q, k].start()
    sib_cp[0, 1].start()

    for pair in range(2):
        blocks = []
        for q in range(4):
            rows = rows_of(pair, q)
            ex = spot(1 - pair, OFFSETS[q])
            w = jnp.concatenate(
                [
                    info[2 * pair, pl.ds(16 + ex, 1), :],
                    info[2 * pair + 1, pl.ds(16 + ex, 1), :],
                ],
                axis=1,
            )
            blocks.append(jnp.where(slot_iota == rows, w, 0.0))
        blocks.append(jnp.zeros((mix_hi.shape[2] - 4 * PAIR, 2 * TOK), F32))
        full = jnp.concatenate(blocks, axis=0).T
        hi = full.astype(BF16)
        mix_hi[pair] = hi
        mix_lo[pair] = (full - hi.astype(F32)).astype(BF16)

    wg_load.wait()
    wu_load.wait()

    y_cp = {}
    back = (0, 3, 1, 2)
    for s in range(1, 4):
        for part in range(2):
            pair = part_at(part, s)
            for k in range(2):
                away = pl.ds(pl.multiple_of((1 - c) * half + k * chunk, 128), chunk)
                y_cp[s, part, k] = remote(
                    x_buf.at[s, part * PAIR : (part + 1) * PAIR, away],
                    ret.at[pair, s * PAIR : (s + 1) * PAIR, chunks[k]],
                    y_s.at[2 * (2 * (s - 1) + part) + k],
                    y_r.at[2 * (pair * 3 + s - 1) + k],
                    dev(part, back[s]),
                )
    hid_tile = 256
    for s in range(4):
        if s == 1:
            for k in range(2):
                for pair in range(2):
                    for q in (1, 2):
                        x_cp[pair, q, k].wait_send()
                for pair in range(2):
                    x_cp[pair, 3, k].start()
        if s > 0:
            for part in range(2):
                for k in range(2):
                    x_cp[part_at(part, s), s, k].wait_recv()
                sib_cp[s, part].start()
        for part in range(2):
            sib_cp[s, part].wait()
        slot = s % 2

        def gate_up(n, carry):
            cols = pl.ds(pl.multiple_of(n * hid_tile, hid_tile), hid_tile)
            rows = x_buf[s]
            g = jnp.dot(rows, wg[:, cols], preferred_element_type=F32) * sg_ref[0:1, cols]
            u = jnp.dot(rows, wu[:, cols], preferred_element_type=F32) * su_ref[0:1, cols]
            h = (g / (1.0 + jnp.exp(-g))) * u
            at = pl.ds(pl.multiple_of(c * ff + n * hid_tile, 128), hid_tile)
            hid[slot, :, at] = h.astype(BF16)
            return carry

        lax.fori_loop(0, ff // hid_tile, gate_up, 0)
        hid_cp = remote(
            hid.at[slot, :, hid_mine],
            hid.at[slot, :, hid_mine],
            hid_s.at[s],
            hid_r.at[s],
            sibling,
        )
        hid_cp.start()
        if s == 0:
            wd_load.wait()
            wd_cp.wait()
        hid_cp.wait()

        def down(n, carry):
            cols = pl.ds(pl.multiple_of(n * tile, tile), tile)
            scale_at = pl.ds(pl.multiple_of(c * half + n * tile, 128), tile)
            y = jnp.dot(hid[slot], wd[:, cols], preferred_element_type=F32)
            y = (y * sd_ref[0:1, scale_at]).astype(BF16)
            if s == 0:
                ret[1, 0:PAIR, cols] = y[0:PAIR]
                ret[0, 0:PAIR, cols] = y[PAIR:]
            else:
                at = pl.ds(pl.multiple_of((1 - c) * half + n * tile, 128), tile)
                x_buf[s, :, at] = y
            return carry

        for k in range(2):
            lax.fori_loop(k * chunk // tile, (k + 1) * chunk // tile, down, 0)
            if s > 0:
                for part in range(2):
                    if s == 3 and k == 1:
                        y_cp[s, part, 0].wait_send()
                    y_cp[s, part, k].start()

    for cp in [tok_cp[2, q] for q in range(4)] + info_cp:
        cp.wait_send()

    def combine(pair, q):
        def step(n, carry):
            cols = pl.ds(pl.multiple_of(n * tile, tile), tile)
            rows = ret[pair, :, cols]
            depth = rows.shape[0]
            total = jnp.dot(mix_hi[pair, :, 0:depth], rows, preferred_element_type=F32)
            total = total + jnp.dot(mix_lo[pair, :, 0:depth], rows, preferred_element_type=F32)
            first, second = total[0:TOK], total[TOK:]
            if pair == 0:
                own[:, cols] = first
                tok[0, TOK:, cols] = second.astype(BF16)
            else:
                passed = relay[:, cols].astype(F32)
                if q % 2 == 0:
                    second = second + passed
                else:
                    first = first + passed
                tok[1, 0:TOK, cols] = first.astype(BF16)
                tok[1, TOK:, cols] = second.astype(BF16)
            return carry

        lax.fori_loop(ends[q] // tile, ends[q + 1] // tile, step, 0)

    relay_cp = [
        remote(
            tok.at[0, TOK : 2 * TOK, quarter[q]],
            relay.at[:, quarter[q]],
            relay_s.at[q],
            relay_r.at[q],
            dev(0, (1, 3)[q % 2]),
        )
        for q in range(4)
    ]
    part_cp = {}
    for i in range(2):
        for k in range(2):
            part_cp[i, k] = remote(
                tok.at[1, i * TOK : (i + 1) * TOK, chunks[k]],
                part_in.at[i, :, chunks[k]],
                part_s.at[2 * i + k],
                part_r.at[2 * i + k],
                dev(1, (3, 1)[i]),
            )

    def wait_rows(pair, k):
        for q in range(1, 4):
            y_cp[q, part_at(pair, q), k].wait_recv()

    for k in range(2):
        wait_rows(0, k)
        for q in (2 * k, 2 * k + 1):
            combine(0, q)
            relay_cp[q].start()
        wait_rows(1, k)
        for q in (2 * k, 2 * k + 1):
            relay_cp[q].wait_recv()
            combine(1, q)
        for i in range(2):
            part_cp[i, k].start()

    def finish(n, carry):
        cols = pl.ds(pl.multiple_of(n * tile, tile), tile)
        total = own[:, cols]
        for i in range(2):
            total = total + part_in[i, :, cols].astype(F32)
        tok[0, 0:TOK, cols] = total.astype(BF16)
        return carry

    stores = []
    for k in range(2):
        for i in range(2):
            part_cp[i, k].wait_recv()
        lax.fori_loop(k * chunk // tile, (k + 1) * chunk // tile, finish, 0)
        store = pltpu.make_async_copy(
            tok.at[0, 0:TOK, chunks[k]], out_hbm.at[:, chunks[k]], loc_sem.at[4 + k]
        )
        store.start()
        stores.append(store)
    for pair in range(2):
        for k in range(2):
            x_cp[pair, 3, k].wait_send()
    for (s, part, k), cp in y_cp.items():
        if s < 3 or k == 1:
            cp.wait_send()
    for cp in [*part_cp.values(), *relay_cp]:
        cp.wait_send()
    for store in stores:
        store.wait()


def body(
    tokens,
    route_expert,
    route_weight,
    gate_weight,
    up_weight,
    down_weight,
    gate_scale,
    up_scale,
    down_scale,
):
    rows, width = tokens.shape
    half = width // 2
    ff = gate_weight.shape[2]
    hbm = pl.BlockSpec(memory_space=pl.ANY)
    vmem = pl.BlockSpec(memory_space=pltpu.VMEM)
    dma = pltpu.SemaphoreType.DMA
    return pl.pallas_call(
        kernel,
        out_shape=jax.ShapeDtypeStruct((rows, half), BF16),
        in_specs=[hbm, vmem, vmem, hbm, hbm, hbm, vmem, vmem, vmem],
        out_specs=hbm,
        scratch_shapes=[
            pltpu.VMEM((4, 2 * PAIR, width), BF16),
            pltpu.VMEM((width, ff), BF16),
            pltpu.VMEM((width, ff), BF16),
            pltpu.VMEM((2 * ff, half), BF16),
            pltpu.VMEM((2, 2 * TOK, half), BF16),
            pltpu.VMEM((2, 3 * PAIR, half), BF16),
            pltpu.VMEM((2, 4 * PAIR, half), BF16),
            pltpu.VMEM((2, 2 * PAIR, 2 * ff), BF16),
            pltpu.VMEM((TOK, half), F32),
            pltpu.VMEM((2, TOK, half), BF16),
            pltpu.VMEM((TOK, half), BF16),
            pltpu.VMEM((4, 32, TOK), F32),
            pltpu.VMEM((2, 4 * PAIR, 2 * TOK), BF16),
            pltpu.VMEM((2, 2 * TOK, 640), BF16),
            pltpu.VMEM((2, 2 * TOK, 640), BF16),
            dma((6,)),
            dma((12,)),
            dma((12,)),
            dma((3,)),
            dma((3,)),
            dma((12,)),
            dma((12,)),
            dma((8,)),
            dma((8,)),
            dma((4,)),
            dma((4,)),
            dma((12,)),
            dma((12,)),
            dma((4,)),
            dma((4,)),
            dma((4,)),
            dma((4,)),
            dma((2,)),
        ],
        compiler_params=pltpu.CompilerParams(
            collective_id=0, has_side_effects=True, vmem_limit_bytes=63 * 2**20
        ),
        name="routed_ffn",
    )(
        tokens,
        route_expert,
        route_weight,
        gate_weight,
        up_weight,
        down_weight,
        gate_scale,
        up_scale,
        down_scale,
    )


def solution(mesh):
    in_specs = (
        P(("dp", "expert"), None),
        P(("dp", "expert"), None),
        P(("dp", "expert"), None),
        P("expert", None, "tensor"),
        P("expert", None, "tensor"),
        P("expert", "tensor", None),
        P("expert", "tensor"),
        P("expert", "tensor"),
        P("expert", None),
    )
    out_specs = P(("dp", "expert"), "tensor")
    return jax.shard_map(body, mesh=mesh, in_specs=in_specs, out_specs=out_specs, check_vma=False)
```

```python
import jax
import jax.numpy as jnp
from jax import lax
from jax.experimental import pallas as pl
from jax.experimental.pallas import tpu as pltpu
from jax.sharding import PartitionSpec as P

ROUTE_SCALE = 2.5
MESH = pl.DeviceIdType.MESH
SIDE = 4
TOK = 128
CAP = 72
PAIR = 2 * CAP
OFFSETS = (0, 1, 3, 2)
BF16 = jnp.bfloat16
F32 = jnp.float32


def kernel(
    tok_hbm,
    re_ref,
    rw_ref,
    wg_hbm,
    wu_hbm,
    wd_hbm,
    sg_ref,
    su_ref,
    sd_ref,
    out_hbm,
    x_buf,
    wg,
    wu,
    wd,
    tok,
    send,
    ret,
    hid,
    own,
    part_in,
    relay,
    info,
    pick,
    mix_hi,
    mix_lo,
    loc_sem,
    tok_s,
    tok_r,
    info_s,
    info_r,
    x_s,
    x_r,
    sib_s,
    sib_r,
    hid_s,
    hid_r,
    y_s,
    y_r,
    part_s,
    part_r,
    relay_s,
    relay_r,
    wd_sem,
):
    half = tok.shape[2]
    ff = wg.shape[1]
    d = lax.axis_index("dp")
    e = lax.axis_index("expert")
    c = lax.axis_index("tensor")
    z, x = e // SIDE, e % SIDE
    odd = (z + x) % 2

    def spot(axis, off):
        along_x = odd if axis == 0 else 1 - odd
        nz = (z + (1 - along_x) * off) % SIDE
        nx = (x + along_x * off) % SIDE
        return nz * SIDE + nx

    def dev(axis, off):
        return (d, spot(axis, off), c)

    sibling = (d, e, 1 - c)
    mine = pl.ds(pl.multiple_of(c * half, 128), half)
    other = pl.ds(pl.multiple_of((1 - c) * half, 128), half)
    hid_mine = pl.ds(pl.multiple_of(c * ff, 128), ff)

    def remote(src, dst, ss, rs, to):
        return pltpu.make_async_remote_copy(
            src_ref=src, dst_ref=dst, send_sem=ss, recv_sem=rs, device_id=to, device_id_type=MESH
        )

    tok_load = pltpu.make_async_copy(tok_hbm.at[:, mine], tok.at[0, 0:TOK], loc_sem.at[0])
    wg_load = pltpu.make_async_copy(wg_hbm.at[0], wg, loc_sem.at[1])
    wu_load = pltpu.make_async_copy(wu_hbm.at[0], wu, loc_sem.at[2])
    wd_load = pltpu.make_async_copy(
        wd_hbm.at[0, :, mine], wd.at[hid_mine], loc_sem.at[3]
    )
    tok_load.start()

    peers = [dev(a, o) for a in (0, 1) for o in (1, 3, 2)] + [sibling]
    barrier = pltpu.get_barrier_semaphore()
    for to in peers:
        pl.semaphore_signal(barrier, inc=1, device_id=to, device_id_type=MESH)
    pl.semaphore_wait(barrier, len(peers))

    chunk = half // 2
    tile = 256
    big = -(-chunk // (2 * tile)) * tile
    ends = (0, big, chunk, 2 * chunk - big, half)
    quarter = [pl.ds(ends[q], ends[q + 1] - ends[q]) for q in range(4)]
    chunks = [pl.ds(k * chunk, chunk) for k in range(2)]

    tok_cp = {}
    for i, off in enumerate((1, 3)):
        for q in range(4):
            tok_cp[i, q] = remote(
                tok_hbm.at[:, pl.ds(pl.multiple_of(c * half + ends[q], 128), ends[q + 1] - ends[q])],
                tok.at[1, i * TOK : (i + 1) * TOK, quarter[q]],
                tok_s.at[4 * i + q],
                tok_r.at[4 * i + q],
                dev(0, off),
            )

    def next_quarter(q):
        if q > 0:
            tok_cp[0, q - 1].wait_send()
            tok_cp[1, (q - 1) ^ 1].wait_send()
        if q < 4:
            tok_cp[0, q].start()
            tok_cp[1, q ^ 1].start()

    next_quarter(0)
    for q in range(4):
        side = q % 2
        tok_cp[2, q] = remote(
            tok.at[1, side * TOK : (side + 1) * TOK, quarter[q]],
            tok.at[0, TOK : 2 * TOK, quarter[q]],
            tok_s.at[8 + q],
            tok_r.at[8 + q],
            dev(1, (1, 3)[side]),
        )
    wg_load.start()
    wu_load.start()
    wd_load.start()
    wd_cp = remote(
        wd_hbm.at[0, :, other], wd.at[hid_mine], wd_sem.at[0], wd_sem.at[1], sibling
    )
    wd_cp.start()

    experts = SIDE * SIDE
    lane = lax.broadcasted_iota(jnp.int32, (TOK, TOK), 1)
    row = lax.broadcasted_iota(jnp.int32, (TOK, TOK), 0)
    wf = rw_ref[...].astype(F32)
    mix = ROUTE_SCALE * wf / jnp.sum(wf, axis=0, keepdims=True)
    expert_row = lax.broadcasted_iota(jnp.int32, (experts, TOK), 0)
    chosen = jnp.zeros((experts, TOK), F32)
    weight = jnp.zeros((experts, TOK), F32)
    for k in range(re_ref.shape[0]):
        hit = re_ref[k : k + 1, :] == expert_row
        chosen = chosen + jnp.where(hit, 1.0, 0.0)
        weight = weight + jnp.where(hit, mix[k : k + 1, :], 0.0)
    before = jnp.where(row < lane, 1.0, 0.0).astype(BF16)
    place = jnp.dot(chosen.astype(BF16), before, preferred_element_type=F32)
    info[0, 0:experts] = jnp.where(chosen > 0.5, place, -1.0)
    info[0, experts : 2 * experts] = weight
    info_cp = [
        remote(
            info.at[0],
            info.at[(2, 3, 1)[i]],
            info_s.at[i],
            info_r.at[i],
            dev(0, (1, 3, 2)[i]),
        )
        for i in range(3)
    ]
    for cp in info_cp:
        cp.start()
    for cp in info_cp:
        cp.wait_recv()

    slot_iota = lax.broadcasted_iota(jnp.int32, (PAIR, 2 * TOK), 0).astype(F32)

    def rows_of(pair, q):
        ex = spot(1 - pair, OFFSETS[q])
        first = info[2 * pair, pl.ds(ex, 1), :]
        second = info[2 * pair + 1, pl.ds(ex, 1), :]
        second = jnp.where(second >= 0.0, second + float(CAP), -1.0)
        return jnp.concatenate([first, second], axis=1)

    for pair in range(2):
        for q in range(4):
            rows = rows_of(pair, q)
            sel = jnp.where(slot_iota == rows, 1.0, 0.0)
            pick[pair, q * PAIR : (q + 1) * PAIR] = sel.astype(BF16)

    def gather(pair, k):
        self_rows = pl.ds((1 - pair) * PAIR, PAIR)

        def step(n, carry):
            cols = pl.ds(pl.multiple_of(n * tile, tile), tile)
            got = jnp.dot(pick[pair], tok[pair, :, cols], preferred_element_type=F32).astype(BF16)
            home = pl.ds(pl.multiple_of(c * half + n * tile, 128), tile)
            x_buf[0, self_rows, home] = got[0:PAIR]
            send[pair, :, cols] = got[PAIR:]
            return carry

        lax.fori_loop(k * chunk // tile, (k + 1) * chunk // tile, step, 0)

    def part_at(pair, q):
        return pair if q < 3 else 1 - pair

    x_cp = {}
    for pair in range(2):
        for q in range(1, 4):
            part = part_at(pair, q)
            for k in range(2):
                home = pl.ds(pl.multiple_of(c * half + k * chunk, 128), chunk)
                x_cp[pair, q, k] = remote(
                    send.at[pair, (q - 1) * PAIR : q * PAIR, chunks[k]],
                    x_buf.at[q, part * PAIR : (part + 1) * PAIR, home],
                    x_s.at[2 * (pair * 3 + q - 1) + k],
                    x_r.at[2 * (2 * (q - 1) + part) + k],
                    dev(1 - pair, OFFSETS[q]),
                )
    sib_cp = {}
    for s in range(4):
        for part in range(2):
            at = x_buf.at[s, part * PAIR : (part + 1) * PAIR, mine]
            sib_cp[s, part] = remote(
                at, at, sib_s.at[2 * s + part], sib_r.at[2 * s + part], sibling
            )

    for k in range(2):
        next_quarter(2 * k + 1)
        for side in range(2):
            tok_cp[side, 2 * k + side].wait_recv()
            tok_cp[2, 2 * k + side].start()
        next_quarter(2 * k + 2)
        for side in range(2):
            tok_cp[side, 2 * k + 1 - side].wait_recv()
        if k == 1:
            for q in (1, 2):
                x_cp[1, q, 0].start()
        gather(1, k)
        if k == 1:
            sib_cp[0, 0].start()
            for q in (1, 2):
                x_cp[1, q, 1].start()
        else:
            tok_load.wait()
        tok_cp[2, 2 * k].wait_recv()
        tok_cp[2, 2 * k + 1].wait_recv()
        gather(0, k)
        for q in (1, 2):
            x_cp[0, q, k].start()
    sib_cp[0, 1].start()

    for pair in range(2):
        blocks = []
        for q in range(4):
            rows = rows_of(pair, q)
            ex = spot(1 - pair, OFFSETS[q])
            w = jnp.concatenate(
                [
                    info[2 * pair, pl.ds(16 + ex, 1), :],
                    info[2 * pair + 1, pl.ds(16 + ex, 1), :],
                ],
                axis=1,
            )
            blocks.append(jnp.where(slot_iota == rows, w, 0.0))
        blocks.append(jnp.zeros((mix_hi.shape[2] - 4 * PAIR, 2 * TOK), F32))
        full = jnp.concatenate(blocks, axis=0).T
        hi = full.astype(BF16)
        mix_hi[pair] = hi
        mix_lo[pair] = (full - hi.astype(F32)).astype(BF16)

    wg_load.wait()
    wu_load.wait()

    y_cp = {}
    back = (0, 3, 1, 2)
    for s in range(1, 4):
        for part in range(2):
            pair = part_at(part, s)
            cuts = (0, chunk, half) if s < 3 else ends
            for k in range(len(cuts) - 1):
                size = cuts[k + 1] - cuts[k]
                away = pl.ds(pl.multiple_of((1 - c) * half + cuts[k], 128), size)
                y_cp[s, part, k] = remote(
                    x_buf.at[s, part * PAIR : (part + 1) * PAIR, away],
                    ret.at[pair, s * PAIR : (s + 1) * PAIR, cuts[k] : cuts[k + 1]],
                    y_s.at[4 * (2 * (s - 1) + part) + k],
                    y_r.at[4 * (pair * 3 + s - 1) + k],
                    dev(part, back[s]),
                )
    hid_tile = 256
    for s in range(4):
        if s == 1:
            for k in range(2):
                for pair in range(2):
                    for q in (1, 2):
                        x_cp[pair, q, k].wait_send()
                for pair in range(2):
                    x_cp[pair, 3, k].start()
        for t in {1: (1, 2), 3: (3,)}.get(s, ()):
            for part in range(2):
                for k in range(2):
                    x_cp[part_at(part, t), t, k].wait_recv()
                sib_cp[t, part].start()
        for part in range(2):
            sib_cp[s, part].wait()
        slot = s % 2

        def gate_up(n, carry):
            cols = pl.ds(pl.multiple_of(n * hid_tile, hid_tile), hid_tile)
            rows = x_buf[s]
            g = jnp.dot(rows, wg[:, cols], preferred_element_type=F32) * sg_ref[0:1, cols]
            u = jnp.dot(rows, wu[:, cols], preferred_element_type=F32) * su_ref[0:1, cols]
            h = (g / (1.0 + jnp.exp(-g))) * u
            at = pl.ds(pl.multiple_of(c * ff + n * hid_tile, 128), hid_tile)
            hid[slot, :, at] = h.astype(BF16)
            return carry

        lax.fori_loop(0, ff // hid_tile, gate_up, 0)
        hid_cp = remote(
            hid.at[slot, :, hid_mine],
            hid.at[slot, :, hid_mine],
            hid_s.at[s],
            hid_r.at[s],
            sibling,
        )
        hid_cp.start()
        if s == 0:
            wd_load.wait()
            wd_cp.wait()
        hid_cp.wait()

        def down(n, carry):
            cols = pl.ds(pl.multiple_of(n * tile, tile), tile)
            scale_at = pl.ds(pl.multiple_of(c * half + n * tile, 128), tile)
            y = jnp.dot(hid[slot], wd[:, cols], preferred_element_type=F32)
            y = (y * sd_ref[0:1, scale_at]).astype(BF16)
            if s == 0:
                ret[1, 0:PAIR, cols] = y[0:PAIR]
                ret[0, 0:PAIR, cols] = y[PAIR:]
            else:
                at = pl.ds(pl.multiple_of((1 - c) * half + n * tile, 128), tile)
                x_buf[s, :, at] = y
            return carry

        if s < 3:
            for k in range(2):
                lax.fori_loop(k * chunk // tile, (k + 1) * chunk // tile, down, 0)
                if s > 0:
                    for part in range(2):
                        y_cp[s, part, k].start()
        else:
            lax.fori_loop(0, ends[1] // tile, down, 0)
            for part in range(2):
                y_cp[s, part, 0].start()
            lax.fori_loop(ends[1] // tile, ends[2] // tile, down, 0)
            for part in range(2):
                y_cp[s, part, 1].start()
            lax.fori_loop(ends[2] // tile, half // tile, down, 0)

    for cp in [tok_cp[2, q] for q in range(4)] + info_cp:
        cp.wait_send()

    def combine(pair, q):
        def step(n, carry):
            cols = pl.ds(pl.multiple_of(n * tile, tile), tile)
            rows = ret[pair, :, cols]
            depth = rows.shape[0]
            total = jnp.dot(mix_hi[pair, :, 0:depth], rows, preferred_element_type=F32)
            total = total + jnp.dot(mix_lo[pair, :, 0:depth], rows, preferred_element_type=F32)
            first, second = total[0:TOK], total[TOK:]
            if pair == 0:
                own[:, cols] = first
                tok[0, TOK:, cols] = second.astype(BF16)
            else:
                passed = relay[:, cols].astype(F32)
                if q % 2 == 0:
                    second = second + passed
                else:
                    first = first + passed
                tok[1, 0:TOK, cols] = first.astype(BF16)
                tok[1, TOK:, cols] = second.astype(BF16)
            return carry

        lax.fori_loop(ends[q] // tile, ends[q + 1] // tile, step, 0)

    relay_cp = [
        remote(
            tok.at[0, TOK : 2 * TOK, quarter[q]],
            relay.at[:, quarter[q]],
            relay_s.at[q],
            relay_r.at[q],
            dev(0, (1, 3)[q % 2]),
        )
        for q in range(4)
    ]
    part_cp = {}
    for i in range(2):
        for q in range(4):
            part_cp[i, q] = remote(
                tok.at[1, i * TOK : (i + 1) * TOK, quarter[q]],
                part_in.at[i, :, quarter[q]],
                part_s.at[4 * i + q],
                part_r.at[4 * i + q],
                dev(1, (3, 1)[i]),
            )

    def wait_rows(pair, q):
        if q % 2 == 0:
            for s in (1, 2):
                y_cp[s, part_at(pair, s), q // 2].wait_recv()
        y_cp[3, part_at(pair, 3), q].wait_recv()

    for q in range(5):
        if q < 2:
            for part in range(2):
                y_cp[3, part, q].wait_send()
                y_cp[3, part, q + 2].start()
        if q < 4:
            wait_rows(0, q)
            combine(0, q)
            relay_cp[q].start()
        if q > 0:
            wait_rows(1, q - 1)
            relay_cp[q - 1].wait_recv()
            combine(1, q - 1)
            for i in range(2):
                part_cp[i, q - 1].start()

    def finish(n, carry):
        cols = pl.ds(pl.multiple_of(n * tile, tile), tile)
        total = own[:, cols]
        for i in range(2):
            total = total + part_in[i, :, cols].astype(F32)
        tok[0, 0:TOK, cols] = total.astype(BF16)
        return carry

    stores = []
    for k in range(2):
        for i in range(2):
            part_cp[i, 2 * k].wait_recv()
            part_cp[i, 2 * k + 1].wait_recv()
        lax.fori_loop(k * chunk // tile, (k + 1) * chunk // tile, finish, 0)
        store = pltpu.make_async_copy(
            tok.at[0, 0:TOK, chunks[k]], out_hbm.at[:, chunks[k]], loc_sem.at[4 + k]
        )
        store.start()
        stores.append(store)
    for pair in range(2):
        for k in range(2):
            x_cp[pair, 3, k].wait_send()
    for (s, part, k), cp in y_cp.items():
        if s < 3 or k > 1:
            cp.wait_send()
    for cp in [*part_cp.values(), *relay_cp]:
        cp.wait_send()
    for store in stores:
        store.wait()


def body(
    tokens,
    route_expert,
    route_weight,
    gate_weight,
    up_weight,
    down_weight,
    gate_scale,
    up_scale,
    down_scale,
):
    rows, width = tokens.shape
    half = width // 2
    ff = gate_weight.shape[2]
    hbm = pl.BlockSpec(memory_space=pl.ANY)
    vmem = pl.BlockSpec(memory_space=pltpu.VMEM)
    dma = pltpu.SemaphoreType.DMA
    return pl.pallas_call(
        kernel,
        out_shape=jax.ShapeDtypeStruct((rows, half), BF16),
        in_specs=[hbm, vmem, vmem, hbm, hbm, hbm, vmem, vmem, vmem],
        out_specs=hbm,
        scratch_shapes=[
            pltpu.VMEM((4, 2 * PAIR, width), BF16),
            pltpu.VMEM((width, ff), BF16),
            pltpu.VMEM((width, ff), BF16),
            pltpu.VMEM((2 * ff, half), BF16),
            pltpu.VMEM((2, 2 * TOK, half), BF16),
            pltpu.VMEM((2, 3 * PAIR, half), BF16),
            pltpu.VMEM((2, 4 * PAIR, half), BF16),
            pltpu.VMEM((2, 2 * PAIR, 2 * ff), BF16),
            pltpu.VMEM((TOK, half), F32),
            pltpu.VMEM((2, TOK, half), BF16),
            pltpu.VMEM((TOK, half), BF16),
            pltpu.VMEM((4, 32, TOK), F32),
            pltpu.VMEM((2, 4 * PAIR, 2 * TOK), BF16),
            pltpu.VMEM((2, 2 * TOK, 640), BF16),
            pltpu.VMEM((2, 2 * TOK, 640), BF16),
            dma((6,)),
            dma((12,)),
            dma((12,)),
            dma((3,)),
            dma((3,)),
            dma((12,)),
            dma((12,)),
            dma((8,)),
            dma((8,)),
            dma((4,)),
            dma((4,)),
            dma((24,)),
            dma((24,)),
            dma((8,)),
            dma((8,)),
            dma((4,)),
            dma((4,)),
            dma((2,)),
        ],
        compiler_params=pltpu.CompilerParams(
            collective_id=0, has_side_effects=True, vmem_limit_bytes=63 * 2**20
        ),
        name="routed_ffn",
    )(
        tokens,
        route_expert.T,
        route_weight.T,
        gate_weight,
        up_weight,
        down_weight,
        gate_scale,
        up_scale,
        down_scale,
    )


def solution(mesh):
    in_specs = (
        P(("dp", "expert"), None),
        P(("dp", "expert"), None),
        P(("dp", "expert"), None),
        P("expert", None, "tensor"),
        P("expert", None, "tensor"),
        P("expert", "tensor", None),
        P("expert", "tensor"),
        P("expert", "tensor"),
        P("expert", None),
    )
    out_specs = P(("dp", "expert"), "tensor")
    return jax.shard_map(body, mesh=mesh, in_specs=in_specs, out_specs=out_specs, check_vma=False)
```

```python
import jax
import jax.numpy as jnp
from jax import lax
from jax.experimental import pallas as pl
from jax.experimental.pallas import tpu as pltpu
from jax.sharding import PartitionSpec as P

ROUTE_SCALE = 2.5
MESH = pl.DeviceIdType.MESH
SIDE = 4
TOK = 128
CAP = 72
PAIR = 2 * CAP
OFFSETS = (0, 1, 3, 2)
BF16 = jnp.bfloat16
F32 = jnp.float32


def kernel(
    tok_hbm,
    re_ref,
    rw_ref,
    wg_hbm,
    wu_hbm,
    wd_hbm,
    sg_ref,
    su_ref,
    sd_ref,
    out_hbm,
    x_buf,
    wg,
    wu,
    wd,
    tok,
    send,
    ret,
    hid,
    own,
    part_in,
    relay,
    info,
    pick,
    mix_hi,
    mix_lo,
    loc_sem,
    tok_s,
    tok_r,
    info_s,
    info_r,
    x_s,
    x_r,
    sib_s,
    sib_r,
    hid_s,
    hid_r,
    y_s,
    y_r,
    part_s,
    part_r,
    relay_s,
    relay_r,
    wd_sem,
):
    half = tok.shape[2]
    ff = wg.shape[1]
    d = lax.axis_index("dp")
    e = lax.axis_index("expert")
    c = lax.axis_index("tensor")
    z, x = e // SIDE, e % SIDE
    odd = (z + x) % 2

    def spot(axis, off):
        along_x = odd if axis == 0 else 1 - odd
        nz = (z + (1 - along_x) * off) % SIDE
        nx = (x + along_x * off) % SIDE
        return nz * SIDE + nx

    def dev(axis, off):
        return (d, spot(axis, off), c)

    sibling = (d, e, 1 - c)
    mine = pl.ds(pl.multiple_of(c * half, 128), half)
    other = pl.ds(pl.multiple_of((1 - c) * half, 128), half)
    hid_mine = pl.ds(pl.multiple_of(c * ff, 128), ff)

    def remote(src, dst, ss, rs, to):
        return pltpu.make_async_remote_copy(
            src_ref=src, dst_ref=dst, send_sem=ss, recv_sem=rs, device_id=to, device_id_type=MESH
        )

    tok_load = pltpu.make_async_copy(tok_hbm.at[:, mine], tok.at[0, 0:TOK], loc_sem.at[0])
    wg_load = pltpu.make_async_copy(wg_hbm.at[0], wg, loc_sem.at[1])
    wu_load = pltpu.make_async_copy(wu_hbm.at[0], wu, loc_sem.at[2])
    wd_load = pltpu.make_async_copy(
        wd_hbm.at[0, :, mine], wd.at[hid_mine], loc_sem.at[3]
    )
    tok_load.start()

    peers = [dev(a, o) for a in (0, 1) for o in (1, 3, 2)] + [sibling]
    barrier = pltpu.get_barrier_semaphore()
    for to in peers:
        pl.semaphore_signal(barrier, inc=1, device_id=to, device_id_type=MESH)
    pl.semaphore_wait(barrier, len(peers))

    chunk = half // 2
    tile = 256
    big = -(-chunk // (2 * tile)) * tile
    ends = (0, big, chunk, 2 * chunk - big, half)
    quarter = [pl.ds(ends[q], ends[q + 1] - ends[q]) for q in range(4)]
    chunks = [pl.ds(k * chunk, chunk) for k in range(2)]

    tok_cp = {}
    for i, off in enumerate((1, 3)):
        for q in range(4):
            tok_cp[i, q] = remote(
                tok_hbm.at[:, pl.ds(pl.multiple_of(c * half + ends[q], 128), ends[q + 1] - ends[q])],
                tok.at[1, i * TOK : (i + 1) * TOK, quarter[q]],
                tok_s.at[4 * i + q],
                tok_r.at[4 * i + q],
                dev(0, off),
            )

    def next_quarter(q):
        if q > 0:
            tok_cp[0, q - 1].wait_send()
            tok_cp[1, (q - 1) ^ 1].wait_send()
        if q < 4:
            tok_cp[0, q].start()
            tok_cp[1, q ^ 1].start()

    next_quarter(0)
    for q in range(4):
        side = q % 2
        tok_cp[2, q] = remote(
            tok.at[1, side * TOK : (side + 1) * TOK, quarter[q]],
            tok.at[0, TOK : 2 * TOK, quarter[q]],
            tok_s.at[8 + q],
            tok_r.at[8 + q],
            dev(1, (1, 3)[side]),
        )
    wg_load.start()
    wu_load.start()
    wd_load.start()
    wd_cp = remote(
        wd_hbm.at[0, :, other], wd.at[hid_mine], wd_sem.at[0], wd_sem.at[1], sibling
    )
    wd_cp.start()

    experts = SIDE * SIDE
    lane = lax.broadcasted_iota(jnp.int32, (TOK, TOK), 1)
    row = lax.broadcasted_iota(jnp.int32, (TOK, TOK), 0)
    wf = rw_ref[...].astype(F32)
    mix = ROUTE_SCALE * wf / jnp.sum(wf, axis=0, keepdims=True)
    expert_row = lax.broadcasted_iota(jnp.int32, (experts, TOK), 0)
    chosen = jnp.zeros((experts, TOK), F32)
    weight = jnp.zeros((experts, TOK), F32)
    for k in range(re_ref.shape[0]):
        hit = re_ref[k : k + 1, :] == expert_row
        chosen = chosen + jnp.where(hit, 1.0, 0.0)
        weight = weight + jnp.where(hit, mix[k : k + 1, :], 0.0)
    before = jnp.where(row < lane, 1.0, 0.0).astype(BF16)
    place = jnp.dot(chosen.astype(BF16), before, preferred_element_type=F32)
    info[0, 0:experts] = jnp.where(chosen > 0.5, place, -1.0)
    info[0, experts : 2 * experts] = weight
    info_cp = [
        remote(
            info.at[0],
            info.at[(2, 3, 1)[i]],
            info_s.at[i],
            info_r.at[i],
            dev(0, (1, 3, 2)[i]),
        )
        for i in range(3)
    ]
    for cp in info_cp:
        cp.start()
    for cp in info_cp:
        cp.wait_recv()

    slot_iota = lax.broadcasted_iota(jnp.int32, (PAIR, 2 * TOK), 0).astype(F32)

    def rows_of(pair, q):
        ex = spot(1 - pair, OFFSETS[q])
        first = info[2 * pair, pl.ds(ex, 1), :]
        second = info[2 * pair + 1, pl.ds(ex, 1), :]
        second = jnp.where(second >= 0.0, second + float(CAP), -1.0)
        return jnp.concatenate([first, second], axis=1)

    for pair in range(2):
        for q in range(4):
            rows = rows_of(pair, q)
            sel = jnp.where(slot_iota == rows, 1.0, 0.0)
            pick[pair, q * PAIR : (q + 1) * PAIR] = sel.astype(BF16)

    def gather(pair, k):
        self_rows = pl.ds((1 - pair) * PAIR, PAIR)

        def step(n, carry):
            cols = pl.ds(pl.multiple_of(n * tile, tile), tile)
            got = jnp.dot(pick[pair], tok[pair, :, cols], preferred_element_type=F32).astype(BF16)
            home = pl.ds(pl.multiple_of(c * half + n * tile, 128), tile)
            x_buf[0, self_rows, home] = got[0:PAIR]
            send[pair, :, cols] = got[PAIR:]
            return carry

        lax.fori_loop(k * chunk // tile, (k + 1) * chunk // tile, step, 0)

    def part_at(pair, q):
        return pair if q < 3 else 1 - pair

    x_cp = {}
    for pair in range(2):
        for q in range(1, 4):
            part = part_at(pair, q)
            for k in range(2):
                home = pl.ds(pl.multiple_of(c * half + k * chunk, 128), chunk)
                x_cp[pair, q, k] = remote(
                    send.at[pair, (q - 1) * PAIR : q * PAIR, chunks[k]],
                    x_buf.at[q, part * PAIR : (part + 1) * PAIR, home],
                    x_s.at[2 * (pair * 3 + q - 1) + k],
                    x_r.at[2 * (2 * (q - 1) + part) + k],
                    dev(1 - pair, OFFSETS[q]),
                )
    sib_cp = {}
    for s in range(4):
        for part in range(2):
            at = x_buf.at[s, part * PAIR : (part + 1) * PAIR, mine]
            sib_cp[s, part] = remote(
                at, at, sib_s.at[2 * s + part], sib_r.at[2 * s + part], sibling
            )

    for k in range(2):
        next_quarter(2 * k + 1)
        for side in range(2):
            tok_cp[side, 2 * k + side].wait_recv()
            tok_cp[2, 2 * k + side].start()
        next_quarter(2 * k + 2)
        for side in range(2):
            tok_cp[side, 2 * k + 1 - side].wait_recv()
        if k == 1:
            for q in (1, 2):
                x_cp[1, q, 0].start()
        gather(1, k)
        if k == 1:
            sib_cp[0, 0].start()
            for q in (1, 2):
                x_cp[1, q, 1].start()
        else:
            tok_load.wait()
        tok_cp[2, 2 * k].wait_recv()
        tok_cp[2, 2 * k + 1].wait_recv()
        gather(0, k)
        for q in (1, 2):
            x_cp[0, q, k].start()
    sib_cp[0, 1].start()

    for pair in range(2):
        blocks = []
        for q in range(4):
            rows = rows_of(pair, q)
            ex = spot(1 - pair, OFFSETS[q])
            w = jnp.concatenate(
                [
                    info[2 * pair, pl.ds(16 + ex, 1), :],
                    info[2 * pair + 1, pl.ds(16 + ex, 1), :],
                ],
                axis=1,
            )
            blocks.append(jnp.where(slot_iota == rows, w, 0.0))
        blocks.append(jnp.zeros((mix_hi.shape[2] - 4 * PAIR, 2 * TOK), F32))
        full = jnp.concatenate(blocks, axis=0).T
        hi = full.astype(BF16)
        mix_hi[pair] = hi
        mix_lo[pair] = (full - hi.astype(F32)).astype(BF16)

    wg_load.wait()
    wu_load.wait()

    y_cp = {}
    back = (0, 3, 1, 2)
    for s in range(1, 4):
        for part in range(2):
            pair = part_at(part, s)
            cuts = (0, chunk, half) if s < 3 else ends
            for k in range(len(cuts) - 1):
                size = cuts[k + 1] - cuts[k]
                away = pl.ds(pl.multiple_of((1 - c) * half + cuts[k], 128), size)
                y_cp[s, part, k] = remote(
                    x_buf.at[s, part * PAIR : (part + 1) * PAIR, away],
                    ret.at[pair, s * PAIR : (s + 1) * PAIR, cuts[k] : cuts[k + 1]],
                    y_s.at[4 * (2 * (s - 1) + part) + k],
                    y_r.at[4 * (pair * 3 + s - 1) + k],
                    dev(part, back[s]),
                )
    hid_tile = 256
    for s in range(4):
        if s == 1:
            for k in range(2):
                for pair in range(2):
                    x_cp[pair, 3, k].start()
        for t in {1: (1, 2), 3: (3,)}.get(s, ()):
            for part in range(2):
                for k in range(2):
                    x_cp[part_at(part, t), t, k].wait_recv()
                sib_cp[t, part].start()
        for part in range(2):
            sib_cp[s, part].wait()
        slot = s % 2

        def gate_up(n, carry):
            cols = pl.ds(pl.multiple_of(n * hid_tile, hid_tile), hid_tile)
            rows = x_buf[s]
            g = jnp.dot(rows, wg[:, cols], preferred_element_type=F32) * sg_ref[0:1, cols]
            u = jnp.dot(rows, wu[:, cols], preferred_element_type=F32) * su_ref[0:1, cols]
            h = (g / (1.0 + jnp.exp(-g))) * u
            at = pl.ds(pl.multiple_of(c * ff + n * hid_tile, 128), hid_tile)
            hid[slot, :, at] = h.astype(BF16)
            return carry

        lax.fori_loop(0, ff // hid_tile, gate_up, 0)
        hid_cp = remote(
            hid.at[slot, :, hid_mine],
            hid.at[slot, :, hid_mine],
            hid_s.at[s],
            hid_r.at[s],
            sibling,
        )
        hid_cp.start()
        if s == 0:
            wd_load.wait()
            wd_cp.wait()
        hid_cp.wait()

        def down(n, carry):
            cols = pl.ds(pl.multiple_of(n * tile, tile), tile)
            scale_at = pl.ds(pl.multiple_of(c * half + n * tile, 128), tile)
            y = jnp.dot(hid[slot], wd[:, cols], preferred_element_type=F32)
            y = (y * sd_ref[0:1, scale_at]).astype(BF16)
            if s == 0:
                ret[1, 0:PAIR, cols] = y[0:PAIR]
                ret[0, 0:PAIR, cols] = y[PAIR:]
            else:
                at = pl.ds(pl.multiple_of((1 - c) * half + n * tile, 128), tile)
                x_buf[s, :, at] = y
            return carry

        if s < 3:
            for k in range(2):
                lax.fori_loop(k * chunk // tile, (k + 1) * chunk // tile, down, 0)
                if s > 0:
                    for part in range(2):
                        y_cp[s, part, k].start()
        else:
            lax.fori_loop(0, ends[1] // tile, down, 0)
            for part in range(2):
                y_cp[s, part, 0].start()
            lax.fori_loop(ends[1] // tile, ends[2] // tile, down, 0)
            for part in range(2):
                y_cp[s, part, 1].start()
            lax.fori_loop(ends[2] // tile, half // tile, down, 0)

    for cp in [tok_cp[2, q] for q in range(4)] + info_cp:
        cp.wait_send()

    def combine(pair, q):
        def step(n, carry):
            cols = pl.ds(pl.multiple_of(n * tile, tile), tile)
            rows = ret[pair, :, cols]
            depth = rows.shape[0]
            total = jnp.dot(mix_hi[pair, :, 0:depth], rows, preferred_element_type=F32)
            total = total + jnp.dot(mix_lo[pair, :, 0:depth], rows, preferred_element_type=F32)
            first, second = total[0:TOK], total[TOK:]
            if pair == 0:
                own[:, cols] = first
                tok[0, TOK:, cols] = second.astype(BF16)
            else:
                passed = relay[:, cols].astype(F32)
                if q % 2 == 0:
                    second = second + passed
                else:
                    first = first + passed
                tok[1, 0:TOK, cols] = first.astype(BF16)
                tok[1, TOK:, cols] = second.astype(BF16)
            return carry

        lax.fori_loop(ends[q] // tile, ends[q + 1] // tile, step, 0)

    relay_cp = [
        remote(
            tok.at[0, TOK : 2 * TOK, quarter[q]],
            relay.at[:, quarter[q]],
            relay_s.at[q],
            relay_r.at[q],
            dev(0, (1, 3)[q % 2]),
        )
        for q in range(4)
    ]
    part_cp = {}
    for i in range(2):
        for q in range(4):
            part_cp[i, q] = remote(
                tok.at[1, i * TOK : (i + 1) * TOK, quarter[q]],
                part_in.at[i, :, quarter[q]],
                part_s.at[4 * i + q],
                part_r.at[4 * i + q],
                dev(1, (3, 1)[i]),
            )

    def wait_rows(pair, q):
        if q % 2 == 0:
            for s in (1, 2):
                y_cp[s, part_at(pair, s), q // 2].wait_recv()
        y_cp[3, part_at(pair, 3), q].wait_recv()

    for q in range(5):
        if q < 2:
            for part in range(2):
                y_cp[3, part, q].wait_send()
                y_cp[3, part, q + 2].start()
        if q < 4:
            wait_rows(0, q)
            combine(0, q)
            relay_cp[q].start()
        if q > 0:
            wait_rows(1, q - 1)
            relay_cp[q - 1].wait_recv()
            combine(1, q - 1)
            for i in range(2):
                part_cp[i, q - 1].start()

    def finish(n, carry):
        cols = pl.ds(pl.multiple_of(n * tile, tile), tile)
        total = own[:, cols]
        for i in range(2):
            total = total + part_in[i, :, cols].astype(F32)
        tok[0, 0:TOK, cols] = total.astype(BF16)
        return carry

    stores = []
    for k in range(2):
        for i in range(2):
            part_cp[i, 2 * k].wait_recv()
            part_cp[i, 2 * k + 1].wait_recv()
        lax.fori_loop(k * chunk // tile, (k + 1) * chunk // tile, finish, 0)
        store = pltpu.make_async_copy(
            tok.at[0, 0:TOK, chunks[k]], out_hbm.at[:, chunks[k]], loc_sem.at[4 + k]
        )
        store.start()
        stores.append(store)
    for cp in x_cp.values():
        cp.wait_send()
    for (s, part, k), cp in y_cp.items():
        if s < 3 or k > 1:
            cp.wait_send()
    for cp in [*part_cp.values(), *relay_cp]:
        cp.wait_send()
    for store in stores:
        store.wait()


def body(
    tokens,
    route_expert,
    route_weight,
    gate_weight,
    up_weight,
    down_weight,
    gate_scale,
    up_scale,
    down_scale,
):
    rows, width = tokens.shape
    half = width // 2
    ff = gate_weight.shape[2]
    hbm = pl.BlockSpec(memory_space=pl.ANY)
    vmem = pl.BlockSpec(memory_space=pltpu.VMEM)
    dma = pltpu.SemaphoreType.DMA
    return pl.pallas_call(
        kernel,
        out_shape=jax.ShapeDtypeStruct((rows, half), BF16),
        in_specs=[hbm, vmem, vmem, hbm, hbm, hbm, vmem, vmem, vmem],
        out_specs=hbm,
        scratch_shapes=[
            pltpu.VMEM((4, 2 * PAIR, width), BF16),
            pltpu.VMEM((width, ff), BF16),
            pltpu.VMEM((width, ff), BF16),
            pltpu.VMEM((2 * ff, half), BF16),
            pltpu.VMEM((2, 2 * TOK, half), BF16),
            pltpu.VMEM((2, 3 * PAIR, half), BF16),
            pltpu.VMEM((2, 4 * PAIR, half), BF16),
            pltpu.VMEM((2, 2 * PAIR, 2 * ff), BF16),
            pltpu.VMEM((TOK, half), F32),
            pltpu.VMEM((2, TOK, half), BF16),
            pltpu.VMEM((TOK, half), BF16),
            pltpu.VMEM((4, 32, TOK), F32),
            pltpu.VMEM((2, 4 * PAIR, 2 * TOK), BF16),
            pltpu.VMEM((2, 2 * TOK, 640), BF16),
            pltpu.VMEM((2, 2 * TOK, 640), BF16),
            dma((6,)),
            dma((12,)),
            dma((12,)),
            dma((3,)),
            dma((3,)),
            dma((12,)),
            dma((12,)),
            dma((8,)),
            dma((8,)),
            dma((4,)),
            dma((4,)),
            dma((24,)),
            dma((24,)),
            dma((8,)),
            dma((8,)),
            dma((4,)),
            dma((4,)),
            dma((2,)),
        ],
        compiler_params=pltpu.CompilerParams(
            collective_id=0, has_side_effects=True, vmem_limit_bytes=63 * 2**20
        ),
        name="routed_ffn",
    )(
        tokens,
        route_expert.T,
        route_weight.T,
        gate_weight,
        up_weight,
        down_weight,
        gate_scale,
        up_scale,
        down_scale,
    )


def solution(mesh):
    in_specs = (
        P(("dp", "expert"), None),
        P(("dp", "expert"), None),
        P(("dp", "expert"), None),
        P("expert", None, "tensor"),
        P("expert", None, "tensor"),
        P("expert", "tensor", None),
        P("expert", "tensor"),
        P("expert", "tensor"),
        P("expert", None),
    )
    out_specs = P(("dp", "expert"), "tensor")
    return jax.shard_map(body, mesh=mesh, in_specs=in_specs, out_specs=out_specs, check_vma=False)
```
